512 devices in a mesh: grp: 8 (over x_hi, y), seq: 64 (over z, x_lo, core).
Axes of the slice: x: 4 (x_hi: 2, x_lo: 2; x = x_hi * 2 + x_lo), y: 4, z: 16, core: 2. Of those that a mesh axis runs over, the one named last changes fastest.
Arguments:
- queries: bfloat16 [65536, 4096], P(('grp', 'seq')), parts along dimension 0, may hold values from -6.5 to 6.5
- resp_key: bfloat16 [65536, 512], P(('grp', 'seq')), parts along dimension 0, may hold values from -6 to 6
- resp_value: bfloat16 [65536, 512], P(('grp', 'seq')), parts along dimension 0, may hold values from -12 to 12
- prompt_key: bfloat16 [4096, 512], P(('grp', 'seq')), parts along dimension 0, may hold values from -6 to 6
- prompt_value: bfloat16 [4096, 512], P(('grp', 'seq')), parts along dimension 0, may hold values from -12 to 12
- out_grad: bfloat16 [65536, 4096], P(('grp', 'seq')), parts along dimension 0, may hold values from -24 to 24
- segment: int32 [65536], P(('grp', 'seq')), parts along dimension 0, may hold values from 0 to 31, never falling along the last dimension, each value on 1 to 385 neighbouring positions
Outputs:
- query_grad: bfloat16 [65536, 4096], P(('grp', 'seq')), parts along dimension 0
- resp_key_grad: float32 [65536, 512], P(('grp', 'seq')), parts along dimension 0
- resp_value_grad: float32 [65536, 512], P(('grp', 'seq')), parts along dimension 0
- prompt_key_grad: float32 [4096, 512], P(('grp', 'seq')), parts along dimension 0
- prompt_value_grad: float32 [4096, 512], P(('grp', 'seq')), parts along dimension 0
The draws below stay inside these ranges and needn't reach their ends.
There are 8 independent parts, one for each index of `grp`. The reference program is written for one: setup_inputs(seed, part) draws one part's arguments, and reference() takes and returns one part's arrays. A program takes and returns all parts, laid end to end along the dimension named above; each array names one. Nothing has to cross between parts.
Inputs may be any that keep to these rules, and one draw needn't show every extreme that they name: segment numbers never fall along the rows; every response holds 1 to 385 tokens, one exactly 385.
All inputs are finite; a program needn't handle non-finite values.
Results may differ from the reference program's by a relative error of at most 0.0059.
Values may be sent and summed in bfloat16 or wider, within the bound.
A program may use at most 64 MiB of HBM per device.

```python
import math
import jax
import jax.numpy as jnp
import numpy as np
from jax import lax

HQ = 32
HK = 4
HD = 128
BACK = 3
ROWS = 128
ROWS_ALL = 8192
PROMPT = 512
RESP = 32
RMAX = 385
N_SEQ = 64


def draw_queries(key, part):
    key = jax.random.fold_in(key, 11)
    base = jnp.clip(jax.random.normal(key, (ROWS_ALL, HQ * HD), jnp.float32), -6.0, 6.0)
    return base.astype(jnp.bfloat16)


def draw_prompt_key(key, part):
    key = jax.random.fold_in(key, 13)
    base = jnp.clip(jax.random.normal(key, (PROMPT, HK * HD), jnp.float32), -6.0, 6.0)
    return base.astype(jnp.bfloat16)


def block_levels(own_key, shape, shards, smallest, top_value):
    factor_of, own = 1.0, jax.random.fold_in(own_key, 6)
    for position, blocks in shards:
        heights = jnp.exp(jax.random.uniform(jax.random.fold_in(own, position), (blocks,), jnp.float32, smallest / len(shards), top_value / len(shards)))
        factor_of = factor_of * jnp.repeat(heights, shape[position] // blocks).reshape([-1 if axis == position else 1 for axis in range(len(shape))])
    return factor_of


def split_up(count, total, limit, slope):
    loads = [(1 << 20) // math.isqrt(grade ** slope) + 1 for grade in range(2, count + 1)]
    surplus, counts = total - limit - (count - 1), [1] * (count - 1)
    while surplus > 0:
        free = [i for i in range(count - 1) if counts[i] < limit]
        pool, budget = sum([loads[i] for i in free]), surplus
        for i in free:
            more = min(limit - counts[i], max(1, budget * loads[i] // pool), surplus)
            counts[i] = counts[i] + more
            surplus = surplus - more
    return np.array([limit] + counts)


def ragged(own_key, number_of, total, limit, skew):
    if number_of == 2:
        one = jax.random.randint(own_key, (), max(1, total - limit), min(limit, total - 1) + 1)
        return jnp.stack([one, total - one])
    tallies = jnp.asarray(split_up(number_of, total, limit, skew), jnp.int32)
    pairs = (number_of - 1) // 2
    donor, receiver = tallies[1:1 + 2 * pairs:2], tallies[2:2 + 2 * pairs:2]
    margin = jnp.minimum(donor - 1, limit - receiver)
    moved = jax.random.randint(jax.random.fold_in(own_key, 1), (pairs,), 0, 1 << 20) % (margin + 1)
    tallies = tallies.at[1:1 + 2 * pairs:2].set(donor - moved).at[2:2 + 2 * pairs:2].set(receiver + moved)
    return tallies[jax.random.permutation(jax.random.fold_in(own_key, 2), number_of)]


def noise(key, dims, spread, most, shards=(), held_as=jnp.bfloat16):
    result = spread * jax.random.normal(key, dims, jnp.float32)
    if shards:
        result = result * block_levels(key, dims, shards, -0.22, 0.18)
    return jnp.clip(result, -most, most).astype(held_as)


def setup_inputs(seed: int = 0, part: int = 0) -> dict:
    keys = jax.random.split(jax.random.key(seed), 8)
    part_splits = jax.random.split(jax.random.fold_in(keys[7], part), 8)
    queries = draw_queries(jax.random.fold_in(jax.random.fold_in(keys[7], part), 71), part)
    resp_key = noise(part_splits[1], (ROWS_ALL, HK * HD), 1.0, 6.0, ((0, 64),))
    resp_value = noise(part_splits[2], (ROWS_ALL, HK * HD), 2.0, 12.0, ((0, 64),))
    prompt_key = draw_prompt_key(jax.random.fold_in(jax.random.fold_in(keys[7], part), 71), part)
    prompt_value = noise(part_splits[4], (PROMPT, HK * HD), 2.0, 12.0, ((0, 64),))
    out_grad = noise(part_splits[5], (ROWS_ALL, HQ * HD), 4.0, 24.0, ((0, 64),))
    segment = jnp.searchsorted(jnp.cumsum(ragged(part_splits[6], RESP, ROWS_ALL, RMAX, 1)), jnp.arange(ROWS_ALL), side="right").astype(jnp.int32)
    return dict(queries=queries, resp_key=resp_key, resp_value=resp_value, prompt_key=prompt_key, prompt_value=prompt_value, out_grad=out_grad, segment=segment)


def float_einsum(form, left, right):
    return jnp.einsum(form, left.astype(jnp.float32), right.astype(jnp.float32), precision=lax.Precision.HIGHEST)


def head_terms(head_queries, head_grads, head_keys, head_values, allowed, scaling, prompt_total):
    scores = float_einsum("rgd,nd->grn", head_queries, head_keys) * scaling
    scores = jnp.where(allowed[None], scores, -jnp.inf)
    highest = jnp.max(scores, axis=2, keepdims=True)
    log_total = highest + jnp.log(jnp.sum(jnp.exp(scores - highest), axis=2, keepdims=True))
    weights = jnp.exp(scores - log_total)
    rounded = lax.optimization_barrier(weights.astype(jnp.bfloat16)).astype(jnp.float32)
    outputs = float_einsum("grn,nd->rgd", rounded, head_values)
    row_delta = jnp.sum(head_grads.astype(jnp.float32) * outputs, axis=2)
    weight_grads = float_einsum("rgd,nd->grn", head_grads, head_values)
    score_grads = weights * (weight_grads - jnp.transpose(row_delta)[:, :, None]) * scaling
    score_grads = lax.optimization_barrier(score_grads.astype(jnp.bfloat16)).astype(jnp.float32)
    grad_query = float_einsum("grn,nd->rgd", score_grads, head_keys)
    grad_keys = float_einsum("grn,rgd->nd", score_grads[:, :, prompt_total:], head_queries)
    grad_values = float_einsum("grn,rgd->nd", rounded[:, :, prompt_total:], head_grads)
    return grad_query, grad_keys, grad_values, score_grads[:, :, :prompt_total], rounded[:, :, :prompt_total]


def attend_block(queries, out_grad, all_keys, all_values, allowed, prompt_total):
    row_count = queries.shape[0]
    group_size = HQ // HK
    scaling = HD ** -0.5
    grad_query, grad_keys, grad_values, score_parts, weight_parts = [], [], [], [], []
    for head_index in range(HK):
        col_lower = head_index * group_size * HD
        col_upper = col_lower + group_size * HD
        head_queries = queries[:, col_lower:col_upper].reshape(row_count, group_size, HD)
        head_grads = out_grad[:, col_lower:col_upper].reshape(row_count, group_size, HD)
        head_keys = all_keys[:, head_index * HD:(head_index + 1) * HD]
        head_values = all_values[:, head_index * HD:(head_index + 1) * HD]
        results = head_terms(head_queries, head_grads, head_keys, head_values, allowed, scaling, prompt_total)
        grad_query.append(results[0].reshape(row_count, group_size * HD))
        grad_keys.append(results[1])
        grad_values.append(results[2])
        score_parts.append(results[3])
        weight_parts.append(results[4])
    return (jnp.concatenate(grad_query, axis=1), jnp.concatenate(grad_keys, axis=1),
            jnp.concatenate(grad_values, axis=1), jnp.stack(score_parts), jnp.stack(weight_parts))


def reference(queries, resp_key, resp_value, prompt_key, prompt_value, out_grad, segment):
    kv_width = HK * HD
    group_size = HQ // HK
    query_blocks = queries.reshape(N_SEQ, ROWS, HQ * HD)
    grad_blocks = out_grad.reshape(N_SEQ, ROWS, HQ * HD)
    key_blocks = resp_key.reshape(N_SEQ, ROWS, kv_width)
    value_blocks = resp_value.reshape(N_SEQ, ROWS, kv_width)
    labels = (segment + 1).reshape(N_SEQ, ROWS).astype(jnp.int32)
    padded_keys = jnp.concatenate((jnp.zeros((BACK, ROWS, kv_width), resp_key.dtype), key_blocks), axis=0)
    padded_values = jnp.concatenate((jnp.zeros((BACK, ROWS, kv_width), resp_value.dtype), value_blocks), axis=0)
    padded_labels = jnp.concatenate((jnp.zeros((BACK, ROWS), jnp.int32), labels), axis=0)
    window_keys = jnp.stack([padded_keys[slot:slot + N_SEQ] for slot in range(BACK)], axis=1)
    window_values = jnp.stack([padded_values[slot:slot + N_SEQ] for slot in range(BACK)], axis=1)
    window_labels = jnp.stack([padded_labels[slot:slot + N_SEQ] for slot in range(BACK)], axis=1)
    row_index = lax.broadcasted_iota(jnp.int32, (ROWS, ROWS), 0)
    col_index = lax.broadcasted_iota(jnp.int32, (ROWS, ROWS), 1)

    def one_block(carried, pieces):
        block_q, block_g, block_k, block_v, win_k, win_v, block_l, win_l = pieces
        masks = [jnp.ones((ROWS, PROMPT), jnp.bool_)]
        for slot in range(BACK):
            masks.append(block_l[:, None] == win_l[slot][None, :])
        masks.append((block_l[:, None] == block_l[None, :]) & (col_index <= row_index))
        allowed = jnp.concatenate(masks, axis=1)
        all_keys = jnp.concatenate((prompt_key, win_k.reshape(BACK * ROWS, kv_width), block_k), axis=0)
        all_values = jnp.concatenate((prompt_value, win_v.reshape(BACK * ROWS, kv_width), block_v), axis=0)
        grad_query, tail_keys, tail_values, score_stack, weight_stack = attend_block(
            block_q, block_g, all_keys, all_values, allowed, PROMPT)
        query_heads = block_q.reshape(ROWS, HK, group_size, HD)
        grad_heads = block_g.reshape(ROWS, HK, group_size, HD)
        key_terms = float_einsum("kgrn,rkgd->nkd", score_stack, query_heads).reshape(PROMPT, kv_width)
        value_terms = float_einsum("kgrn,rkgd->nkd", weight_stack, grad_heads).reshape(PROMPT, kv_width)
        return (carried[0] + key_terms, carried[1] + value_terms), (grad_query.astype(jnp.bfloat16), tail_keys, tail_values)

    start_sums = (jnp.zeros((PROMPT, kv_width), jnp.float32), jnp.zeros((PROMPT, kv_width), jnp.float32))
    prompt_sums, outputs = lax.scan(one_block, start_sums, (query_blocks, grad_blocks, key_blocks, value_blocks,
                                                           window_keys, window_values, labels, window_labels))
    grad_query, tail_keys, tail_values = outputs
    tail_keys = tail_keys.reshape(N_SEQ, BACK + 1, ROWS, kv_width)
    tail_values = tail_values.reshape(N_SEQ, BACK + 1, ROWS, kv_width)
    zero_tail = jnp.zeros((BACK, BACK + 1, ROWS, kv_width), jnp.float32)
    padded_tk = jnp.concatenate((tail_keys, zero_tail), axis=0)
    padded_tv = jnp.concatenate((tail_values, zero_tail), axis=0)
    key_grad = jnp.zeros((N_SEQ, ROWS, kv_width), jnp.float32)
    value_grad = jnp.zeros((N_SEQ, ROWS, kv_width), jnp.float32)
    for slot in range(BACK + 1):
        lower = BACK - slot
        key_grad = key_grad + padded_tk[lower:lower + N_SEQ, slot]
        value_grad = value_grad + padded_tv[lower:lower + N_SEQ, slot]
    return (grad_query.reshape(ROWS_ALL, HQ * HD), key_grad.reshape(ROWS_ALL, kv_width),
            value_grad.reshape(ROWS_ALL, kv_width), prompt_sums[0], prompt_sums[1])
```

```python
import math

import jax
import jax.numpy as jnp
from jax import lax
from jax.experimental import pallas as pl
from jax.experimental.pallas import tpu as pltpu
from jax.sharding import PartitionSpec as P

MESH = pl.DeviceIdType.MESH
HD = 128
HK = 4
GROUP = 8
PAIRS = GROUP // 2
SCALE = HD ** (-0.5)
EXP_SCALE = SCALE * math.log2(math.e)
BF = jnp.bfloat16
F32 = jnp.float32


def body(
    nz,
    q_ref,
    rk_ref,
    rv_ref,
    pk_ref,
    pv_ref,
    do_ref,
    seg_ref,
    dq_ref,
    drk_ref,
    drv_ref,
    dpk_ref,
    dpv_ref,
    qt,
    dot,
    win,
    gat,
    bias,
    pr,
    dpr,
    mr,
    lr,
    sp,
    dpp,
    kp,
    vp,
    kt,
    pt,
    dst,
    ps,
    pf,
    rc,
    xs,
    xf,
    rx,
    zs,
    zf,
    rz,
    tb,
    tf,
    rp,
    ts,
    ra,
    rb,
    s_kv,
    r_kv,
    s_one,
    r_one,
):
    n = 4 * nz
    keys = 4 * HD
    npr = 32 * nz
    total = keys + npr
    me = lax.axis_index("seq")
    grp = lax.axis_index("grp")
    core = me % 2
    x = (me // 2) % 2
    z = me // 4
    peer = me + 1 - 2 * core
    xpeer = me + 2 - 4 * x

    def zpeer(d):
        return ((z + d) % nz) * 4 + me % 4

    def device(index):
        return (grp, index)

    GZ, GX, GC, PC, PX, PZ, TP, TB, TA = range(9)

    def copy(src, dst, kind, g, to):
        return pltpu.make_async_remote_copy(
            src_ref=src,
            dst_ref=dst,
            send_sem=s_one.at[kind, g],
            recv_sem=r_one.at[kind, g],
            device_id=device(to),
            device_id_type=MESH,
        )

    barrier = pltpu.get_barrier_semaphore()

    def greet(to):
        pl.semaphore_signal(barrier, inc=1, device_id=device(to), device_id_type=MESH)

    greet(peer)
    greet(xpeer)
    greet((me + 2) % n)
    greet((me + n - 2) % n)
    greet((me + n + 6 * core - 3) % n)

    def greet_z(d, carry):
        greet(zpeer(d))
        return carry

    lax.fori_loop(1, nz, greet_z, 0)

    labels = jnp.broadcast_to((seg_ref[...] + 1).astype(F32), (16, HD)).astype(BF)
    for g in range(HK):
        cols = slice(g * HD, (g + 1) * HD)
        win[g, 0, 0:HD, :] = rk_ref[:, cols]
        win[g, 0, HD : 2 * HD, :] = rv_ref[:, cols]
        win[g, 0, 2 * HD : 2 * HD + 16, :] = labels
        gat[g, core, x, z] = jnp.concatenate(
            (pk_ref[:, cols].astype(F32), pv_ref[:, cols].astype(F32)), axis=0
        ).astype(BF)
    pl.semaphore_wait(barrier, 5 + nz - 1)

    def block(g, slot):
        return win.at[g, slot, pl.ds(0, 2 * HD + (16 if g == 0 else 0))]

    def kv_copy(g, which, from_slot, to_slot, to):
        return pltpu.make_async_remote_copy(
            src_ref=block(g, from_slot),
            dst_ref=block(g, to_slot),
            send_sem=s_kv.at[g, which],
            recv_sem=r_kv.at[g, to_slot],
            device_id=device(to),
            device_id_type=MESH,
        )

    def kv_far(g):
        return kv_copy(g, 0, 0, 2, (me + 2) % n)

    def kv_side(g):
        return kv_copy(g, 1, 0, 1 + 2 * core, (me + 1 + 2 * core) % n)

    def kv_pass(g):
        return kv_copy(g, 2, 2, 3 - 2 * core, peer)

    def kv_forward(g):
        kv_far(g).wait_recv()
        kv_pass(g).start()

    def kv_ready(g):
        kv_copy(g, 1, 0, 1, peer).wait_recv()
        kv_copy(g, 1, 0, 3, peer).wait_recv()

    def gz_start(g):
        def step(d, carry):
            copy(gat.at[g, core, x, z], gat.at[g, core, x, z], GZ, g, zpeer(d)).start()
            return carry

        lax.fori_loop(1, nz, step, 0)

    def gz_all(g):
        part = gat.at[g, core, x, pl.ds(0, nz - 1)]
        return copy(part, part, GZ, g, peer)

    def gx_copy(g):
        return copy(gat.at[g, core, x], gat.at[g, core, x], GX, g, xpeer)

    def gc_copy(g):
        return copy(gat.at[g, core], gat.at[g, core], GC, g, peer)

    def gather_x(g):
        gz_all(g).wait_recv()
        gx_copy(g).start()

    def gather_c(g):
        gx_copy(g).wait_recv()
        gc_copy(g).start()

    for g in range(HK):
        kv_far(g).start()
        kv_side(g).start()
        gz_start(g)

    def flip(h, carry):
        cols = pl.ds(pl.multiple_of(h * HD, HD), HD)
        qt[:, cols] = q_ref[:, cols].T
        dot[:, cols] = do_ref[:, cols].T
        return carry

    lax.fori_loop(0, HK * GROUP, flip, 0)

    def make_bias():
        mine = jnp.broadcast_to(win[0, 0, 2 * HD : 2 * HD + 16, :].astype(F32)[0:1], (HD, HD))
        row = lax.broadcasted_iota(jnp.int32, (HD, HD), 1)
        col = lax.broadcasted_iota(jnp.int32, (HD, HD), 0)
        for slot in range(4):
            theirs = jnp.broadcast_to(
                win[0, slot, 2 * HD : 2 * HD + 16, :].astype(F32)[0:1], (HD, HD)
            ).T
            seen = mine == theirs
            if slot == 0:
                seen = seen & (col <= row)
            else:
                seen = seen & (jnp.broadcast_to(me, (HD, HD)) >= slot)
            bias[slot] = jnp.where(seen, 0.0, -jnp.inf)

    def fold(value, op):
        return op(value.reshape(value.shape[0] // 8, 8, value.shape[1]), axis=0)

    def unit_cols(g, u):
        return pl.ds(pl.multiple_of((g * PAIRS + u) * 2 * HD, 2 * HD), 2 * HD)

    def resp_unit(g, u):
        unit = g * PAIRS + u
        cols = unit_cols(g, u)
        q2 = qt[:, cols]
        do2 = dot[:, cols]
        high = None
        for slot in range(4):
            mask = bias[slot]
            part = jnp.dot(win[g, slot, 0:HD, :], q2, preferred_element_type=F32)
            part = part + jnp.concatenate((mask, mask), axis=1)
            pr[unit, slot] = part
            top = fold(part, jnp.max)
            high = top if high is None else jnp.maximum(high, top)
            dpr[unit, slot] = jnp.dot(
                win[g, slot, HD : 2 * HD, :], do2, preferred_element_type=F32
            )
        high = jnp.max(high, axis=0, keepdims=True)
        low = None
        for slot in range(4):
            part = jnp.exp2((pr[unit, slot] - high) * EXP_SCALE)
            pr[unit, slot] = part
            add = fold(part, jnp.sum)
            low = add if low is None else low + add
        mr[unit] = jnp.broadcast_to(high, (8, 2 * HD))
        lr[unit] = jnp.broadcast_to(jnp.sum(low, axis=0, keepdims=True), (8, 2 * HD))

    def prompt_ready(g):
        gc_copy(g).wait_recv()
        all_rows = gat[g].reshape(4 * nz, 16, HD).astype(F32)
        kp[...] = all_rows[:, 0:8].reshape(npr, HD).astype(BF)
        vp[...] = all_rows[:, 8:16].reshape(npr, HD).astype(BF)
        for slot in range(4):
            kt[:, slot * HD : (slot + 1) * HD] = win[g, slot, 0:HD, :].T
        for lower in range(0, npr, HD):
            width = min(HD, npr - lower)
            kt[:, keys + lower : keys + lower + width] = kp[lower : lower + width, :].T

    chunk = min(HD, npr)
    chunks = npr // chunk

    def full_unit(g, u):
        unit = g * PAIRS + u
        cols = unit_cols(g, u)
        own = pl.ds(pl.multiple_of(u * 2 * HD, 2 * HD), 2 * HD)
        q2 = qt[:, cols]
        do2 = dot[:, cols]
        high = mr[unit]
        for c in range(chunks):
            rows = slice(c * chunk, (c + 1) * chunk)
            part = jnp.dot(kp[rows, :], q2, preferred_element_type=F32)
            sp[rows, :] = part
            high = jnp.maximum(high, fold(part, jnp.max))
            dpp[rows, :] = jnp.dot(vp[rows, :], do2, preferred_element_type=F32)
        old = mr[unit][0:1]
        high = jnp.max(high, axis=0, keepdims=True)
        low = None
        for c in range(chunks):
            rows = slice(c * chunk, (c + 1) * chunk)
            part = jnp.exp2((sp[rows, :] - high) * EXP_SCALE)
            sp[rows, :] = part
            add = fold(part, jnp.sum)
            low = add if low is None else low + add
        shrink = jnp.exp2((old - high) * EXP_SCALE)
        sums = jnp.sum(low, axis=0, keepdims=True) + lr[unit][0:1] * shrink
        f_prompt = 1.0 / sums
        f_resp = shrink * f_prompt
        delta = None
        for slot in range(4):
            rounded = (pr[unit, slot] * f_resp).astype(BF)
            pt[slot * HD : (slot + 1) * HD, own] = rounded
            add = fold(rounded.astype(F32) * dpr[unit, slot], jnp.sum)
            delta = add if delta is None else delta + add
        for c in range(chunks):
            rows = slice(c * chunk, (c + 1) * chunk)
            rounded = (sp[rows, :] * f_prompt).astype(BF)
            pt[keys + c * chunk : keys + (c + 1) * chunk, own] = rounded
            delta = delta + fold(rounded.astype(F32) * dpp[rows, :], jnp.sum)
        delta = jnp.sum(delta, axis=0, keepdims=True)
        for slot in range(4):
            dst[slot * HD : (slot + 1) * HD, own] = (
                (pr[unit, slot] * f_resp) * (dpr[unit, slot] - delta)
            ).astype(BF)
        for c in range(chunks):
            rows = slice(c * chunk, (c + 1) * chunk)
            dst[keys + c * chunk : keys + (c + 1) * chunk, own] = (
                (sp[rows, :] * f_prompt) * (dpp[rows, :] - delta)
            ).astype(BF)

    def head_grads(g):
        heads = range(g * GROUP, (g + 1) * GROUP)
        q_rows = jnp.concatenate([q_ref[:, h * HD : (h + 1) * HD] for h in heads], axis=0)
        do_rows = jnp.concatenate([do_ref[:, h * HD : (h + 1) * HD] for h in heads], axis=0)
        for lower in range(0, npr, chunk):
            rows = slice(keys + lower, keys + lower + chunk)
            dk = jnp.dot(dst[rows, :], q_rows, preferred_element_type=F32) * SCALE
            dv = jnp.dot(pt[rows, :], do_rows, preferred_element_type=F32)
            blocks = chunk // 8
            both = jnp.concatenate(
                (dk.reshape(blocks, 8, HD), dv.reshape(blocks, 8, HD)), axis=1
            )
            first = lower // 8
            pf[g, first : first + blocks] = both
            ps[g, first : first + blocks] = both.astype(BF)
        pc_copy(g).start()
        for slot in range(4):
            rows = slice(slot * HD, (slot + 1) * HD)
            dk = jnp.dot(dst[rows, :], q_rows, preferred_element_type=F32) * SCALE
            dv = jnp.dot(pt[rows, :], do_rows, preferred_element_type=F32)
            if slot in (0, 2):
                tf[g, slot // 2, 0:HD, :] = dk
                tf[g, slot // 2, HD : 2 * HD, :] = dv
            else:
                tb[g, slot // 2, 0:HD, :] = dk.astype(BF)
                tb[g, slot // 2, HD : 2 * HD, :] = dv.astype(BF)
        tp_copy(g).start()
        tb_copy(g).start()

    def head_query(g):
        for j in range(PAIRS):
            part = jnp.dot(
                kt[...], dst[:, j * 2 * HD : (j + 1) * 2 * HD], preferred_element_type=F32
            )
            for i in range(2):
                h = g * GROUP + j * 2 + i
                dq_ref[:, h * HD : (h + 1) * HD] = (
                    part[:, i * HD : (i + 1) * HD].T * SCALE
                ).astype(BF)

    half = 2 * nz

    def pc_copy(g):
        return copy(ps.at[g, pl.ds((1 - core) * half, half)], rc.at[g], PC, g, peer)

    def px_copy(g):
        return copy(xs.at[g], rx.at[g], PX, g, xpeer)

    def px_send(g):
        pc_copy(g).wait_recv()
        away = 1 - x
        xs[g] = (
            pf[g, pl.ds(core * half + away * nz, nz)]
            + rc[g, pl.ds(away * nz, nz)].astype(F32)
        ).astype(BF)
        xf[g] = pf[g, pl.ds(core * half + x * nz, nz)] + rc[g, pl.ds(x * nz, nz)].astype(F32)
        px_copy(g).start()

    def pz_send(g):
        px_copy(g).wait_recv()
        sums = xf[g] + rx[g].astype(F32)
        zf[g] = sums
        zs[g] = sums.astype(BF)

        def step(d, carry):
            copy(zs.at[g, (z + d) % nz], rz.at[g, d - 1], PZ, g, zpeer(d)).start()
            return carry

        lax.fori_loop(1, nz, step, 0)

    def pz_all(g):
        return copy(zs.at[g, pl.ds(0, nz - 1)], rz.at[g], PZ, g, peer)

    def prompt_out(g):
        pz_all(g).wait_recv()
        sums = zf[g, z] + jnp.sum(rz[g].astype(F32), axis=0)
        cols = slice(g * HD, (g + 1) * HD)
        dpk_ref[:, cols] = sums[0:8]
        dpv_ref[:, cols] = sums[8:16]

    def tp_copy(g):
        return copy(tb.at[g, core], rp.at[g], TP, g, peer)

    def tb_copy(g):
        return copy(tb.at[g, 1 - core], rb.at[g], TB, g, (me + n - 3 + 2 * core) % n)

    def ta_copy(g):
        return copy(ts.at[g], ra.at[g], TA, g, (me + n - 2) % n)

    def ts_send(g):
        tp_copy(g).wait_recv()
        ts[g] = (tf[g, 1] + rp[g].astype(F32)).astype(BF)
        ta_copy(g).start()

    def resp_out(g):
        ta_copy(g).wait_recv()
        tb_copy(g).wait_recv()
        sums = tf[g, 0] + ra[g].astype(F32) + rb[g].astype(F32)
        cols = slice(g * HD, (g + 1) * HD)
        drk_ref[:, cols] = sums[0:HD]
        drv_ref[:, cols] = sums[HD : 2 * HD]

    def run(unit, g, lower, upper):
        def step(u, carry):
            unit(g, u)
            return carry

        lax.fori_loop(lower, upper, step, 0)

    kv_forward(0)
    for g in range(HK):
        if g + 1 < HK:
            kv_forward(g + 1)
        kv_ready(g)
        if g == 0:
            make_bias()
        run(resp_unit, g, 0, PAIRS)
        if g >= 2:
            gather_c(g - 2)
        if g >= 1:
            gather_x(g - 1)
    for g in range(HK):
        if g == 1:
            gather_c(HK - 1)
        prompt_ready(g)
        run(full_unit, g, 0, 2)
        if g == 0:
            gather_c(HK - 2)
            gather_x(HK - 1)
        else:
            px_send(g - 1)
            ts_send(g - 1)
        run(full_unit, g, 2, PAIRS)
        if g > 0:
            pz_send(g - 1)
        head_grads(g)
        head_query(g)
    last = HK - 1
    px_send(last)
    ts_send(last)
    for g in range(last):
        prompt_out(g)
        resp_out(g)
    pz_send(last)
    resp_out(last)
    prompt_out(last)

    for g in range(HK):
        kv_far(g).wait_send()
        kv_side(g).wait_send()
        kv_pass(g).wait_send()
        gz_all(g).wait_send()
        gx_copy(g).wait_send()
        gc_copy(g).wait_send()
        pc_copy(g).wait_send()
        px_copy(g).wait_send()
        pz_all(g).wait_send()
        tp_copy(g).wait_send()
        tb_copy(g).wait_send()
        ta_copy(g).wait_send()


def on_device(queries, resp_key, resp_value, prompt_key, prompt_value, out_grad, segment):
    n = lax.axis_size("seq")
    nz = n // 4
    rows = queries.shape[0]
    npr = 32 * nz
    total = 4 * HD + npr
    units = HK * PAIRS
    vmem = pl.BlockSpec(memory_space=pltpu.VMEM)
    scratch = [
        ((HD, HK * GROUP * HD), BF),
        ((HD, HK * GROUP * HD), BF),
        ((HK, 4, 2 * HD + 16, HD), BF),
        ((HK, 2, 2, nz, 16, HD), BF),
        ((4, HD, HD), F32),
        ((units, 4, HD, 2 * HD), F32),
        ((units, 4, HD, 2 * HD), F32),
        ((units, 8, 2 * HD), F32),
        ((units, 8, 2 * HD), F32),
        ((npr, 2 * HD), F32),
        ((npr, 2 * HD), F32),
        ((npr, HD), BF),
        ((npr, HD), BF),
        ((HD, total), BF),
        ((total, GROUP * HD), BF),
        ((total, GROUP * HD), BF),
        ((HK, 4 * nz, 16, HD), BF),
        ((HK, 4 * nz, 16, HD), F32),
        ((HK, 2 * nz, 16, HD), BF),
        ((HK, nz, 16, HD), BF),
        ((HK, nz, 16, HD), F32),
        ((HK, nz, 16, HD), BF),
        ((HK, nz, 16, HD), BF),
        ((HK, nz, 16, HD), F32),
        ((HK, nz - 1, 16, HD), BF),
        ((HK, 2, 2 * HD, HD), BF),
        ((HK, 2, 2 * HD, HD), F32),
        ((HK, 2 * HD, HD), BF),
        ((HK, 2 * HD, HD), BF),
        ((HK, 2 * HD, HD), BF),
        ((HK, 2 * HD, HD), BF),
    ]
    return tuple(
        pl.pallas_call(
            lambda *refs: body(nz, *refs),
            out_shape=[
                jax.ShapeDtypeStruct((rows, HK * GROUP * HD), BF),
                jax.ShapeDtypeStruct((rows, HK * HD), F32),
                jax.ShapeDtypeStruct((rows, HK * HD), F32),
                jax.ShapeDtypeStruct((8, HK * HD), F32),
                jax.ShapeDtypeStruct((8, HK * HD), F32),
            ],
            in_specs=[vmem] * 7,
            out_specs=[vmem] * 5,
            scratch_shapes=[pltpu.VMEM(shape, kind) for shape, kind in scratch]
            + [
                pltpu.SemaphoreType.DMA((HK, 3)),
                pltpu.SemaphoreType.DMA((HK, 4)),
                pltpu.SemaphoreType.DMA((9, HK)),
                pltpu.SemaphoreType.DMA((9, HK)),
            ],
            compiler_params=pltpu.CompilerParams(
                collective_id=0, has_side_effects=True, vmem_limit_bytes=56 * 1024 * 1024
            ),
            cost_estimate=pl.CostEstimate(
                flops=6 * 10**9, bytes_accessed=6 * 10**6, transcendentals=4 * 10**6
            ),
            name="attention_backward",
        )(
            queries,
            resp_key,
            resp_value,
            prompt_key,
            prompt_value,
            out_grad,
            segment.reshape(1, rows),
        )
    )


def solution(mesh):
    spec = P(("grp", "seq"), None)
    return jax.shard_map(
        on_device,
        mesh=mesh,
        in_specs=(spec,) * 6 + (P(("grp", "seq")),),
        out_specs=(spec,) * 5,
        check_vma=False,
    )
```

```python
import math

import jax
import jax.numpy as jnp
from jax import lax
from jax.experimental import pallas as pl
from jax.experimental.pallas import tpu as pltpu
from jax.sharding import PartitionSpec as P

MESH = pl.DeviceIdType.MESH
HD = 128
HK = 4
GROUP = 8
PAIRS = GROUP // 2
SCALE = HD ** (-0.5)
EXP_SCALE = SCALE * math.log2(math.e)
BF = jnp.bfloat16
F32 = jnp.float32


def body(
    nz,
    q_hbm,
    rk_ref,
    rv_ref,
    pk_ref,
    pv_ref,
    do_hbm,
    seg_ref,
    dq_hbm,
    drk_ref,
    drv_ref,
    dpk_ref,
    dpv_ref,
    q_ref,
    do_ref,
    dq_ref,
    qt,
    dot,
    win,
    gat,
    bias,
    pr_a,
    pr_b,
    dpr_a,
    dpr_b,
    mr,
    lr,
    sp_a,
    sp_b,
    dpp_a,
    dpp_b,
    kp,
    vp,
    kt,
    pt,
    dst,
    dk_acc,
    dv_acc,
    ps,
    pf,
    rc,
    xs,
    xf,
    rx,
    zs,
    zf,
    rz,
    tb,
    tf,
    rp,
    ts,
    ra,
    rb,
    s_kv,
    r_kv,
    s_ring,
    r_ring,
    s_one,
    r_one,
    s_in,
    s_out,
):
    n = 4 * nz
    keys = 4 * HD
    npr = 32 * nz
    total = keys + npr
    quads = 2 * HK
    wide = 4 * HD
    me = lax.axis_index("seq")
    grp = lax.axis_index("grp")
    core = lax.rem(me, 2)
    x = lax.rem(lax.div(me, 2), 2)
    z = lax.div(me, 4)
    peer = me + 1 - 2 * core
    xpeer = me + 2 - 4 * x

    def zpeer(d):
        return lax.rem(me + 4 * d, n)

    def device(index):
        return (grp, index)

    GX, GC, PC, PX, PZ, TP, TB, TA = range(8)

    def copy(src, dst, kind, g, to):
        return pltpu.make_async_remote_copy(
            src_ref=src,
            dst_ref=dst,
            send_sem=s_one.at[kind, g],
            recv_sem=r_one.at[kind, g],
            device_id=device(to),
            device_id_type=MESH,
        )

    barrier = pltpu.get_barrier_semaphore()

    def greet(to):
        pl.semaphore_signal(barrier, inc=1, device_id=device(to), device_id_type=MESH)

    greet(peer)
    greet(xpeer)
    greet(lax.rem(me + 2, n))
    greet(lax.rem(me + n - 2, n))
    greet(lax.rem(me + n + 6 * core - 3, n))

    def greet_z(d, carry):
        greet(zpeer(d))
        return carry

    lax.fori_loop(1, nz, greet_z, 0)
    q_in = pltpu.make_async_copy(q_hbm, q_ref, s_in.at[0])
    do_in = pltpu.make_async_copy(do_hbm, do_ref, s_in.at[1])
    q_in.start()
    do_in.start()

    labels = jnp.broadcast_to((seg_ref[...] + 1).astype(F32), (16, HD)).astype(BF)
    for g in range(HK):
        cols = slice(g * HD, (g + 1) * HD)
        win[g, 0, 0:HD, :] = rk_ref[:, cols]
        win[g, 0, HD : 2 * HD, :] = rv_ref[:, cols]
        win[g, 0, 2 * HD : 2 * HD + 16, :] = labels
        gat[core, x, z, g] = jnp.concatenate(
            (pk_ref[:, cols].astype(F32), pv_ref[:, cols].astype(F32)), axis=0
        ).astype(BF)
    pl.semaphore_wait(barrier, 5 + nz - 1)

    def kv_copy(g, which, from_slot, to_slot, to):
        return pltpu.make_async_remote_copy(
            src_ref=win.at[g, from_slot],
            dst_ref=win.at[g, to_slot],
            send_sem=s_kv.at[g, which],
            recv_sem=r_kv.at[g, to_slot],
            device_id=device(to),
            device_id_type=MESH,
        )

    def kv_far(g):
        return kv_copy(g, 0, 0, 2, lax.rem(me + 2, n))

    def kv_side(g):
        return kv_copy(g, 1, 0, 1 + 2 * core, lax.rem(me + 1 + 2 * core, n))

    def kv_pass(g):
        return kv_copy(g, 2, 2, 3 - 2 * core, peer)

    def kv_forward(g):
        kv_far(g).wait_recv()
        kv_pass(g).start()

    def kv_ready(g):
        kv_copy(g, 1, 0, 1, peer).wait_recv()
        kv_copy(g, 1, 0, 3, peer).wait_recv()

    steps = nz // 4

    def ring_copy(owner, to, d):
        part = gat.at[core, x, owner]
        return pltpu.make_async_remote_copy(
            src_ref=part,
            dst_ref=part,
            send_sem=s_ring.at[0],
            recv_sem=r_ring.at[d],
            device_id=device(to),
            device_id_type=MESH,
        )

    def ring_wait(d):
        ring_copy(lax.rem(z + nz - d, nz), peer, d).wait_recv()

    def ring_step(k):
        if k > 1:
            ring_wait(2 * (k - 1))
            ring_wait(nz - 2 * (k - 1))
        up = lax.rem(z + nz - 2 * (k - 1), nz)
        down = lax.rem(z + 2 * (k - 1), nz)
        ring_copy(up, zpeer(2), 2 * k).start()
        if k < steps:
            ring_copy(down, zpeer(nz - 2), nz - 2 * k).start()
        ring_copy(up, zpeer(1), 2 * k - 1).start()
        ring_copy(down, zpeer(nz - 1), nz - 2 * k + 1).start()

    def gx_copy(g):
        part = gat.at[core, x, pl.ds(0, nz), g]
        return copy(part, part, GX, g, xpeer)

    def gc_copy(g):
        part = gat.at[core, pl.ds(0, 2), pl.ds(0, nz), g]
        return copy(part, part, GC, g, peer)

    def ring_end():
        for k in range(1, steps + 1):
            ring_wait(2 * k - 1)
            ring_wait(nz - 2 * k + 1)
        ring_wait(2 * steps)

    def gather_x(g):
        gx_copy(g).start()

    def gather_c(g):
        gx_copy(g).wait_recv()
        gc_copy(g).start()

    def kv_send(g):
        kv_far(g).start()
        kv_side(g).start()

    kv_send(0)
    ring_step(1)
    kv_send(1)

    q_in.wait()
    do_in.wait()

    def flip(h, carry):
        for i in range(4):
            cols = pl.ds(pl.multiple_of((h * 4 + i) * HD, HD), HD)
            qt[:, cols] = q_ref[:, cols].T
            dot[:, cols] = do_ref[:, cols].T
        return carry

    lax.fori_loop(0, HK * GROUP // 8, flip, 0)
    ring_step(2)
    lax.fori_loop(HK * GROUP // 8, HK * GROUP // 4, flip, 0)
    kv_forward(0)
    ring_step(3)

    def make_bias():
        mine = jnp.broadcast_to(win[0, 0, 2 * HD : 2 * HD + 16, :].astype(F32)[0:1], (HD, HD))
        row = lax.broadcasted_iota(jnp.int32, (HD, HD), 1)
        col = lax.broadcasted_iota(jnp.int32, (HD, HD), 0)
        for slot in range(4):
            theirs = jnp.broadcast_to(
                win[0, slot, 2 * HD : 2 * HD + 16, :].astype(F32)[0:1], (HD, HD)
            ).T
            seen = mine == theirs
            if slot == 0:
                seen = seen & (col <= row)
            else:
                seen = seen & (jnp.broadcast_to(me, (HD, HD)) >= slot)
            bias[slot] = jnp.where(seen, 0.0, -jnp.inf)

    def fold(value, op):
        return op(value.reshape(value.shape[0] // 8, 8, value.shape[1]), axis=0)

    def half_cols(quad, half):
        return pl.ds(pl.multiple_of(quad * wide + half * 2 * HD, 2 * HD), 2 * HD)

    def quad_cols(quad):
        return pl.ds(pl.multiple_of(quad * wide, wide), wide)

    def resp_half(quad, half, pr, dpr):
        g = lax.div(quad, 2)
        cols = half_cols(quad, half)
        k4 = win[g, :, 0:HD, :].reshape(keys, HD)
        v4 = win[g, :, HD : 2 * HD, :].reshape(keys, HD)
        scores = jnp.dot(k4, qt[:, cols], preferred_element_type=F32)
        high = None
        for slot in range(4):
            mask = bias[slot]
            part = scores[slot * HD : (slot + 1) * HD] + jnp.concatenate((mask, mask), axis=1)
            pr[quad, slot] = part
            top = fold(part, jnp.max)
            high = top if high is None else jnp.maximum(high, top)
        high = jnp.max(high, axis=0, keepdims=True)
        dpr[quad] = jnp.dot(v4, dot[:, cols], preferred_element_type=F32).reshape(4, HD, 2 * HD)
        low = None
        for slot in range(4):
            part = jnp.exp2((pr[quad, slot] - high) * EXP_SCALE)
            pr[quad, slot] = part
            add = fold(part, jnp.sum)
            low = add if low is None else low + add
        mr[quad, half] = jnp.broadcast_to(high, (8, 2 * HD))
        lr[quad, half] = jnp.broadcast_to(jnp.sum(low, axis=0, keepdims=True), (8, 2 * HD))

    def prompt_ready(g):
        gc_copy(g).wait_recv()
        all_rows = gat[:, :, :, g].reshape(4 * nz, 16, HD).astype(F32)
        kp[g] = all_rows[:, 0:8].reshape(npr, HD).astype(BF)
        vp[g] = all_rows[:, 8:16].reshape(npr, HD).astype(BF)
        for slot in range(4):
            kt[g, :, slot * HD : (slot + 1) * HD] = win[g, slot, 0:HD, :].T
        for lower in range(0, npr, HD):
            kt[g, :, keys + lower : keys + lower + HD] = kp[g, lower : lower + HD, :].T

    chunks = npr // HD

    def full_half(quad, half, pr, dpr, sp, dpp):
        g = lax.div(quad, 2)
        cols = half_cols(quad, half)
        own = slice(half * 2 * HD, (half + 1) * 2 * HD)
        scores = jnp.dot(kp[g], qt[:, cols], preferred_element_type=F32)
        sp[...] = scores
        high = jnp.maximum(mr[quad, half], fold(scores, jnp.max))
        dpp[...] = jnp.dot(vp[g], dot[:, cols], preferred_element_type=F32)
        old = mr[quad, half][0:1]
        high = jnp.max(high, axis=0, keepdims=True)
        low = None
        for c in range(chunks):
            rows = slice(c * HD, (c + 1) * HD)
            part = jnp.exp2((sp[rows, :] - high) * EXP_SCALE)
            sp[rows, :] = part
            add = fold(part, jnp.sum)
            low = add if low is None else low + add
        shrink = jnp.exp2((old - high) * EXP_SCALE)
        sums = jnp.sum(low, axis=0, keepdims=True) + lr[quad, half][0:1] * shrink
        f_prompt = 1.0 / sums
        f_resp = shrink * f_prompt
        delta = None
        for slot in range(4):
            rounded = (pr[quad, slot] * f_resp).astype(BF)
            pt[slot * HD : (slot + 1) * HD, own] = rounded
            add = fold(rounded.astype(F32) * dpr[quad, slot], jnp.sum)
            delta = add if delta is None else delta + add
        for c in range(chunks):
            rows = slice(c * HD, (c + 1) * HD)
            rounded = (sp[rows, :] * f_prompt).astype(BF)
            pt[keys + c * HD : keys + (c + 1) * HD, own] = rounded
            delta = delta + fold(rounded.astype(F32) * dpp[rows, :], jnp.sum)
        delta = jnp.sum(delta, axis=0, keepdims=True)
        for slot in range(4):
            dst[slot * HD : (slot + 1) * HD, own] = (
                (pr[quad, slot] * f_resp) * (dpr[quad, slot] - delta)
            ).astype(BF)
        for c in range(chunks):
            rows = slice(c * HD, (c + 1) * HD)
            dst[keys + c * HD : keys + (c + 1) * HD, own] = (
                (sp[rows, :] * f_prompt) * (dpp[rows, :] - delta)
            ).astype(BF)

    def full_quad(quad):
        full_half(quad, 0, pr_a, dpr_a, sp_a, dpp_a)
        full_half(quad, 1, pr_b, dpr_b, sp_b, dpp_b)

    def rows_of(ref, quad):
        part = ref[:, quad_cols(quad)]
        return jnp.concatenate([part[:, i * HD : (i + 1) * HD] for i in range(4)], axis=0)

    def add_keys(quad, lower, upper):
        second = lax.rem(quad, 2) == 1
        rows = slice(lower, upper)
        for acc, left, right in ((dv_acc, pt, do_ref), (dk_acc, dst, q_ref)):
            part = jnp.dot(left[rows, :], rows_of(right, quad), preferred_element_type=F32)
            acc[rows, :] = jnp.where(second, acc[rows, :], 0.0) + part

    def query_part(quad):
        g = lax.div(quad, 2)
        part = jnp.dot(kt[g], dst[...], preferred_element_type=F32)
        dq_ref[:, quad_cols(quad)] = jnp.concatenate(
            [(part[:, i * HD : (i + 1) * HD].T * SCALE).astype(BF) for i in range(4)], axis=1
        )

    def query_out(quad):
        cols = quad_cols(quad)
        return pltpu.make_async_copy(dq_ref.at[:, cols], dq_hbm.at[:, cols], s_out.at[quad])

    def emit_prompt(g):
        dk = dk_acc[keys:total, :] * SCALE
        dv = dv_acc[keys:total, :]
        both = jnp.concatenate(
            (dk.reshape(4 * nz, 8, HD), dv.reshape(4 * nz, 8, HD)), axis=1
        )
        pf[g] = both
        ps[g] = both.astype(BF)
        pc_copy(g).start()

    def emit_resp(g):
        for slot in range(4):
            rows = slice(slot * HD, (slot + 1) * HD)
            dk = dk_acc[rows, :] * SCALE
            dv = dv_acc[rows, :]
            if slot in (0, 2):
                tf[g, slot // 2, 0:HD, :] = dk
                tf[g, slot // 2, HD : 2 * HD, :] = dv
            else:
                tb[g, slot // 2, 0:HD, :] = dk.astype(BF)
                tb[g, slot // 2, HD : 2 * HD, :] = dv.astype(BF)
        tp_copy(g).start()
        tb_copy(g).start()

    half_blocks = 2 * nz

    def pc_copy(g):
        return copy(
            ps.at[g, pl.ds((1 - core) * half_blocks, half_blocks)], rc.at[g], PC, g, peer
        )

    def px_copy(g):
        return copy(xs.at[g], rx.at[g], PX, g, xpeer)

    def px_send(g):
        pc_copy(g).wait_recv()
        away = 1 - x
        xs[g] = (
            pf[g, pl.ds(core * half_blocks + away * nz, nz)]
            + rc[g, pl.ds(away * nz, nz)].astype(F32)
        ).astype(BF)
        xf[g] = (
            pf[g, pl.ds(core * half_blocks + x * nz, nz)] + rc[g, pl.ds(x * nz, nz)].astype(F32)
        )
        px_copy(g).start()

    def pz_send(g):
        px_copy(g).wait_recv()
        sums = xf[g] + rx[g].astype(F32)
        zf[g] = sums
        zs[g] = sums.astype(BF)

        for d in range(1, nz):
            copy(zs.at[g, lax.rem(z + d, nz)], rz.at[g, d - 1], PZ, g, zpeer(d)).start()

    def pz_all(g):
        return copy(zs.at[g, pl.ds(0, nz - 1)], rz.at[g], PZ, g, peer)

    def prompt_out(g):
        pz_all(g).wait_recv()
        sums = zf[g, z] + jnp.sum(rz[g].astype(F32), axis=0)
        cols = slice(g * HD, (g + 1) * HD)
        dpk_ref[:, cols] = sums[0:8]
        dpv_ref[:, cols] = sums[8:16]

    def tp_copy(g):
        return copy(tb.at[g, core], rp.at[g], TP, g, peer)

    def tb_copy(g):
        return copy(tb.at[g, 1 - core], rb.at[g], TB, g, lax.rem(me + n - 3 + 2 * core, n))

    def ta_copy(g):
        return copy(ts.at[g], ra.at[g], TA, g, lax.rem(me + n - 2, n))

    def ts_send(g):
        tp_copy(g).wait_recv()
        ts[g] = (tf[g, 1] + rp[g].astype(F32)).astype(BF)
        ta_copy(g).start()

    def resp_out(g):
        ta_copy(g).wait_recv()
        tb_copy(g).wait_recv()
        sums = tf[g, 0] + ra[g].astype(F32) + rb[g].astype(F32)
        cols = slice(g * HD, (g + 1) * HD)
        drk_ref[:, cols] = sums[0:HD]
        drv_ref[:, cols] = sums[HD : 2 * HD]

    def when(flag, *calls):
        @pl.when(flag)
        def _():
            for call, g in calls:
                call(g)

    def resp_quad(quad):
        resp_half(quad, 0, pr_a, dpr_a)
        resp_half(quad, 1, pr_b, dpr_b)

    kv_ready(0)
    make_bias()

    def resp_step(quad, carry):
        when(quad == 2, (kv_ready, 1))
        resp_quad(quad)
        when(quad == 0, (ring_step, 4), (kv_forward, 1))

        @pl.when(quad == 1)
        def _():
            ring_end()
            gather_x(0)
            kv_send(2)

        when(quad == 2, (gather_x, 1))
        when(quad == 3, (gather_c, 0), (kv_forward, 2), (kv_send, 3))
        return carry

    lax.fori_loop(0, 4, resp_step, 0)
    kv_ready(2)
    prompt_ready(0)
    resp_quad(4)
    full_quad(0)
    gather_c(1)
    gather_x(2)

    def both_step(quad, carry):
        when(quad == 6, (kv_ready, 3), (prompt_ready, 1))
        add_keys(quad - 5, 0, total)
        query_part(quad - 5)
        resp_quad(quad)
        full_quad(quad - 4)
        query_out(quad - 5).start()
        when(quad == 5, (kv_forward, 3), (gather_x, 3))
        when(quad == 6, (emit_prompt, 0), (emit_resp, 0), (gather_c, 2))
        when(quad == 7, (gather_c, 3), (px_send, 0), (ts_send, 0))
        return carry

    lax.fori_loop(5, quads, both_step, 0)

    def full_step(quad, carry):
        g = lax.div(quad, 2)
        first = lax.rem(quad, 2) == 0
        when(first, (prompt_ready, g))
        add_keys(quad - 1, 0, total)
        query_part(quad - 1)
        full_quad(quad)
        query_out(quad - 1).start()
        when(first, (emit_prompt, g - 1), (emit_resp, g - 1), (pz_send, g - 2))
        when(~first, (px_send, g - 1), (ts_send, g - 1))
        return carry

    lax.fori_loop(4, quads, full_step, 0)
    last = HK - 1
    add_keys(quads - 1, keys, total)
    emit_prompt(last)
    pz_send(last - 1)
    add_keys(quads - 1, 0, keys)
    emit_resp(last)
    query_part(quads - 1)
    query_out(quads - 1).start()
    px_send(last)
    ts_send(last)
    for g in range(last):
        prompt_out(g)
        resp_out(g)
    pz_send(last)
    resp_out(last)
    prompt_out(last)

    sent = gat.at[0, 0, pl.ds(0, nz - 1)]
    pltpu.make_async_remote_copy(
        src_ref=sent,
        dst_ref=sent,
        send_sem=s_ring.at[0],
        recv_sem=r_ring.at[0],
        device_id=device(peer),
        device_id_type=MESH,
    ).wait_send()
    for g in range(HK):
        kv_far(g).wait_send()
        kv_side(g).wait_send()
        kv_pass(g).wait_send()
        gx_copy(g).wait_send()
        gc_copy(g).wait_send()
        pc_copy(g).wait_send()
        px_copy(g).wait_send()
        pz_all(g).wait_send()
        tp_copy(g).wait_send()
        tb_copy(g).wait_send()
        ta_copy(g).wait_send()
    for quad in range(quads):
        query_out(quad).wait()


def hand_over(*refs):
    sems = refs[10]
    copies = [
        pltpu.make_async_copy(refs[i], refs[5 + i], sems.at[i]) for i in range(5)
    ]
    for one in copies:
        one.start()
    for one in copies:
        one.wait()


def on_device(queries, resp_key, resp_value, prompt_key, prompt_value, out_grad, segment):
    n = lax.axis_size("seq")
    nz = n // 4
    rows = queries.shape[0]
    npr = 32 * nz
    total = 4 * HD + npr
    quads = 2 * HK
    vmem = pl.BlockSpec(memory_space=pltpu.VMEM)
    whole = pl.BlockSpec(memory_space=pl.ANY)
    flat = HK * GROUP * HD
    scratch = [
        ((rows, flat), BF),
        ((rows, flat), BF),
        ((rows, flat), BF),
        ((HD, flat), BF),
        ((HD, flat), BF),
        ((HK, 4, 2 * HD + 16, HD), BF),
        ((2, 2, nz, HK, 16, HD), BF),
        ((4, HD, HD), F32),
        ((quads, 4, HD, 2 * HD), F32),
        ((quads, 4, HD, 2 * HD), F32),
        ((quads, 4, HD, 2 * HD), F32),
        ((quads, 4, HD, 2 * HD), F32),
        ((quads, 2, 8, 2 * HD), F32),
        ((quads, 2, 8, 2 * HD), F32),
        ((npr, 2 * HD), F32),
        ((npr, 2 * HD), F32),
        ((npr, 2 * HD), F32),
        ((npr, 2 * HD), F32),
        ((HK, npr, HD), BF),
        ((HK, npr, HD), BF),
        ((HK, HD, total), BF),
        ((total, 4 * HD), BF),
        ((total, 4 * HD), BF),
        ((total, HD), F32),
        ((total, HD), F32),
        ((HK, 4 * nz, 16, HD), BF),
        ((HK, 4 * nz, 16, HD), F32),
        ((HK, 2 * nz, 16, HD), BF),
        ((HK, nz, 16, HD), BF),
        ((HK, nz, 16, HD), F32),
        ((HK, nz, 16, HD), BF),
        ((HK, nz, 16, HD), BF),
        ((HK, nz, 16, HD), F32),
        ((HK, nz - 1, 16, HD), BF),
        ((HK, 2, 2 * HD, HD), BF),
        ((HK, 2, 2 * HD, HD), F32),
        ((HK, 2 * HD, HD), BF),
        ((HK, 2 * HD, HD), BF),
        ((HK, 2 * HD, HD), BF),
        ((HK, 2 * HD, HD), BF),
    ]
    shapes = [
        jax.ShapeDtypeStruct((rows, flat), BF),
        jax.ShapeDtypeStruct((rows, HK * HD), F32),
        jax.ShapeDtypeStruct((rows, HK * HD), F32),
        jax.ShapeDtypeStruct((8, HK * HD), F32),
        jax.ShapeDtypeStruct((8, HK * HD), F32),
    ]
    results = pl.pallas_call(
        lambda *refs: body(nz, *refs),
        out_shape=shapes,
        in_specs=[whole] + [vmem] * 4 + [whole, vmem],
        out_specs=[whole] + [vmem] * 4,
        scratch_shapes=[pltpu.VMEM(shape, kind) for shape, kind in scratch]
        + [
            pltpu.SemaphoreType.DMA((HK, 3)),
            pltpu.SemaphoreType.DMA((HK, 4)),
            pltpu.SemaphoreType.DMA((1,)),
            pltpu.SemaphoreType.DMA((nz,)),
            pltpu.SemaphoreType.DMA((8, HK)),
            pltpu.SemaphoreType.DMA((8, HK)),
            pltpu.SemaphoreType.DMA((2,)),
            pltpu.SemaphoreType.DMA((quads,)),
        ],
        compiler_params=pltpu.CompilerParams(
            collective_id=0, has_side_effects=True, vmem_limit_bytes=60 * 1024 * 1024
        ),
        cost_estimate=pl.CostEstimate(
            flops=6 * 10**9, bytes_accessed=6 * 10**6, transcendentals=4 * 10**6
        ),
        name="attention_backward",
    )(
        queries,
        resp_key,
        resp_value,
        prompt_key,
        prompt_value,
        out_grad,
        segment.reshape(1, rows),
    )
    return tuple(
        pl.pallas_call(
            hand_over,
            out_shape=shapes,
            in_specs=[vmem] * 5,
            out_specs=[whole] * 5,
            scratch_shapes=[pltpu.SemaphoreType.DMA((5,))],
            cost_estimate=pl.CostEstimate(
                flops=0, bytes_accessed=3 * 10**6, transcendentals=0
            ),
            name="hand_over",
        )(*results)
    )


def solution(mesh):
    spec = P(("grp", "seq"), None)
    return jax.shard_map(
        on_device,
        mesh=mesh,
        in_specs=(spec,) * 6 + (P(("grp", "seq")),),
        out_specs=(spec,) * 5,
        check_vma=False,
    )
```

```python
import jax
import jax.numpy as jnp
from jax import lax
from jax.experimental import pallas as pl
from jax.experimental.pallas import tpu as pltpu
from jax.sharding import PartitionSpec as P

MESH = pl.DeviceIdType.MESH
HD = 128
HK = 4
GROUP = 8
PAIRS = GROUP // 2
SCALE = HD ** (-0.5)
BF = jnp.bfloat16
F32 = jnp.float32


def gather_body(
    nz, rk_ref, rv_ref, pk_ref, pv_ref, seg_ref, win, gat, s_kv, r_kv, s_ring, r_ring, s_one, r_one
):
    n = 4 * nz
    keys = 4 * HD
    npr = 32 * nz
    total = keys + npr
    me = lax.axis_index("seq")
    grp = lax.axis_index("grp")
    core = lax.rem(me, 2)
    x = lax.rem(lax.div(me, 2), 2)
    z = lax.div(me, 4)
    peer = me + 1 - 2 * core
    xpeer = me + 2 - 4 * x

    def zpeer(d):
        return lax.rem(me + 4 * d, n)

    def device(index):
        return (grp, index)

    def copy(src, dst, kind, g, to):
        return pltpu.make_async_remote_copy(
            src_ref=src,
            dst_ref=dst,
            send_sem=s_one.at[kind, g],
            recv_sem=r_one.at[kind, g],
            device_id=device(to),
            device_id_type=MESH,
        )

    barrier = pltpu.get_barrier_semaphore()

    def greet(to):
        pl.semaphore_signal(barrier, inc=1, device_id=device(to), device_id_type=MESH)

    greet(peer)
    greet(xpeer)
    greet(lax.rem(me + 2, n))
    greet(lax.rem(me + n - 2, n))
    greet(lax.rem(me + n + 6 * core - 3, n))

    for d in (1, 2, nz - 1, nz - 2):
        greet(zpeer(d))

    labels = jnp.broadcast_to((seg_ref[...] + 1).astype(F32), (16, HD)).astype(BF)
    for g in range(HK):
        cols = slice(g * HD, (g + 1) * HD)
        win[g, 0, 0:HD, :] = rk_ref[:, cols]
        win[g, 0, HD : 2 * HD, :] = rv_ref[:, cols]
        win[g, 0, 2 * HD : 2 * HD + 16, :] = labels
        gat[core, x, z, g] = jnp.concatenate(
            (pk_ref[:, cols].astype(F32), pv_ref[:, cols].astype(F32)), axis=0
        ).astype(BF)
    pl.semaphore_wait(barrier, 9)
    GX, GC = range(2)

    def kv_copy(g, which, from_slot, to_slot, to):
        return pltpu.make_async_remote_copy(
            src_ref=win.at[g, from_slot],
            dst_ref=win.at[g, to_slot],
            send_sem=s_kv.at[g, which],
            recv_sem=r_kv.at[g, to_slot],
            device_id=device(to),
            device_id_type=MESH,
        )

    def kv_far(g):
        return kv_copy(g, 0, 0, 2, lax.rem(me + 2, n))

    def kv_side(g):
        return kv_copy(g, 1, 0, 1 + 2 * core, lax.rem(me + 1 + 2 * core, n))

    def kv_pass(g):
        return kv_copy(g, 2, 2, 3 - 2 * core, peer)

    def kv_forward(g):
        kv_far(g).wait_recv()
        kv_pass(g).start()

    def kv_ready(g):
        kv_copy(g, 1, 0, 1, peer).wait_recv()
        kv_copy(g, 1, 0, 3, peer).wait_recv()

    steps = nz // 4

    def ring_copy(owner, to, d):
        part = gat.at[core, x, owner]
        return pltpu.make_async_remote_copy(
            src_ref=part,
            dst_ref=part,
            send_sem=s_ring.at[0],
            recv_sem=r_ring.at[d],
            device_id=device(to),
            device_id_type=MESH,
        )

    def ring_wait(d):
        ring_copy(lax.rem(z + nz - d, nz), peer, d).wait_recv()

    def ring_step(k):
        if k > 1:
            ring_wait(2 * (k - 1))
            ring_wait(nz - 2 * (k - 1))
        up = lax.rem(z + nz - 2 * (k - 1), nz)
        down = lax.rem(z + 2 * (k - 1), nz)
        ring_copy(up, zpeer(2), 2 * k).start()
        if k < steps:
            ring_copy(down, zpeer(nz - 2), nz - 2 * k).start()
        ring_copy(up, zpeer(1), 2 * k - 1).start()
        ring_copy(down, zpeer(nz - 1), nz - 2 * k + 1).start()

    def gx_copy(g):
        part = gat.at[core, x, pl.ds(0, nz), g]
        return copy(part, part, GX, g, xpeer)

    def gc_copy(g):
        part = gat.at[core, pl.ds(0, 2), pl.ds(0, nz), g]
        return copy(part, part, GC, g, peer)

    def ring_end():
        for k in range(1, steps + 1):
            ring_wait(2 * k - 1)
            ring_wait(nz - 2 * k + 1)
        ring_wait(2 * steps)

    def kv_send(g):
        kv_far(g).start()
        kv_side(g).start()

    kv_send(0)
    ring_step(1)
    for g in range(1, HK):
        kv_send(g)
    kv_forward(0)
    ring_step(2)
    kv_forward(1)
    ring_step(3)
    kv_forward(2)
    ring_step(4)
    kv_forward(3)
    ring_end()
    for g in range(HK):
        gx_copy(g).start()
    for g in range(HK):
        gx_copy(g).wait_recv()
        gc_copy(g).start()
    for g in range(HK):
        kv_ready(g)
    for g in range(HK):
        gc_copy(g).wait_recv()
    sent = gat.at[0, 0, pl.ds(0, nz - 1)]
    pltpu.make_async_remote_copy(
        src_ref=sent,
        dst_ref=sent,
        send_sem=s_ring.at[0],
        recv_sem=r_ring.at[0],
        device_id=device(peer),
        device_id_type=MESH,
    ).wait_send()
    for g in range(HK):
        for one in (kv_far, kv_side, kv_pass, gx_copy, gc_copy):
            one(g).wait_send()


def compute_body(
    nz,
    q_hbm,
    do_hbm,
    win,
    gat,
    dq_hbm,
    pf,
    tf,
    q_ref,
    do_ref,
    dq_ref,
    qt,
    dot,
    bias,
    pr_a,
    pr_b,
    dpr_a,
    dpr_b,
    mr,
    lr,
    sp_a,
    sp_b,
    dpp_a,
    dpp_b,
    kp,
    vp,
    kt,
    pt,
    dst,
    dk_acc,
    dv_acc,
    s_in,
    s_out,
):
    keys = 4 * HD
    npr = 32 * nz
    total = keys + npr
    quads = 2 * HK
    wide = 4 * HD
    me = lax.axis_index("seq")
    q_in = pltpu.make_async_copy(q_hbm, q_ref, s_in.at[0])
    do_in = pltpu.make_async_copy(do_hbm, do_ref, s_in.at[1])
    q_in.start()
    do_in.start()
    q_in.wait()
    do_in.wait()

    def flip(h, carry):
        for i in range(4):
            cols = pl.ds(pl.multiple_of((h * 4 + i) * HD, HD), HD)
            qt[:, cols] = q_ref[:, cols].T
            dot[:, cols] = do_ref[:, cols].T
        return carry

    lax.fori_loop(0, HK * GROUP // 4, flip, 0)

    def make_bias():
        mine = jnp.broadcast_to(win[0, 0, 2 * HD : 2 * HD + 16, :].astype(F32)[0:1], (HD, HD))
        row = lax.broadcasted_iota(jnp.int32, (HD, HD), 1)
        col = lax.broadcasted_iota(jnp.int32, (HD, HD), 0)
        for slot in range(4):
            theirs = jnp.broadcast_to(
                win[0, slot, 2 * HD : 2 * HD + 16, :].astype(F32)[0:1], (HD, HD)
            ).T
            seen = mine == theirs
            if slot == 0:
                seen = seen & (col <= row)
            else:
                seen = seen & (jnp.broadcast_to(me, (HD, HD)) >= slot)
            bias[slot] = jnp.where(seen, 0.0, -jnp.inf)

    def fold(value, op):
        return op(value.reshape(value.shape[0] // 8, 8, value.shape[1]), axis=0)

    def half_cols(quad, half):
        return pl.ds(pl.multiple_of(quad * wide + half * 2 * HD, 2 * HD), 2 * HD)

    def quad_cols(quad):
        return pl.ds(pl.multiple_of(quad * wide, wide), wide)

    def resp_half(quad, half, pr, dpr):
        g = lax.div(quad, 2)
        cols = half_cols(quad, half)
        k4 = win[g, :, 0:HD, :].reshape(keys, HD)
        v4 = win[g, :, HD : 2 * HD, :].reshape(keys, HD)
        scores = jnp.dot(k4, qt[:, cols], preferred_element_type=F32)
        high = None
        for slot in range(4):
            mask = bias[slot]
            part = scores[slot * HD : (slot + 1) * HD] + jnp.concatenate((mask, mask), axis=1)
            pr[quad, slot] = part
            top = fold(part, jnp.max)
            high = top if high is None else jnp.maximum(high, top)
        high = jnp.max(high, axis=0, keepdims=True)
        dpr[quad] = jnp.dot(v4, dot[:, cols], preferred_element_type=F32).reshape(4, HD, 2 * HD)
        low = None
        for slot in range(4):
            part = jnp.exp((pr[quad, slot] - high) * SCALE)
            pr[quad, slot] = part
            add = fold(part, jnp.sum)
            low = add if low is None else low + add
        mr[quad, half] = jnp.broadcast_to(high, (8, 2 * HD))
        lr[quad, half] = jnp.broadcast_to(jnp.sum(low, axis=0, keepdims=True), (8, 2 * HD))

    def prompt_ready(g):
        all_rows = gat[:, :, :, g].reshape(4 * nz, 16, HD).astype(F32)
        kp[g] = all_rows[:, 0:8].reshape(npr, HD).astype(BF)
        vp[g] = all_rows[:, 8:16].reshape(npr, HD).astype(BF)
        for slot in range(4):
            kt[g, :, slot * HD : (slot + 1) * HD] = win[g, slot, 0:HD, :].T
        for lower in range(0, npr, HD):
            kt[g, :, keys + lower : keys + lower + HD] = kp[g, lower : lower + HD, :].T

    chunks = npr // HD

    def full_half(quad, half, pr, dpr, sp, dpp):
        g = lax.div(quad, 2)
        cols = half_cols(quad, half)
        own = slice(half * 2 * HD, (half + 1) * 2 * HD)
        scores = jnp.dot(kp[g], qt[:, cols], preferred_element_type=F32)
        sp[...] = scores
        high = jnp.maximum(mr[quad, half], fold(scores, jnp.max))
        dpp[...] = jnp.dot(vp[g], dot[:, cols], preferred_element_type=F32)
        old = mr[quad, half][0:1]
        high = jnp.max(high, axis=0, keepdims=True)
        low = None
        for c in range(chunks):
            rows = slice(c * HD, (c + 1) * HD)
            part = jnp.exp((sp[rows, :] - high) * SCALE)
            sp[rows, :] = part
            add = fold(part, jnp.sum)
            low = add if low is None else low + add
        shrink = jnp.exp((old - high) * SCALE)
        sums = jnp.sum(low, axis=0, keepdims=True) + lr[quad, half][0:1] * shrink
        f_prompt = 1.0 / sums
        f_resp = shrink * f_prompt
        delta = None
        for slot in range(4):
            rounded = (pr[quad, slot] * f_resp).astype(BF)
            pt[slot * HD : (slot + 1) * HD, own] = rounded
            add = fold(rounded.astype(F32) * dpr[quad, slot], jnp.sum)
            delta = add if delta is None else delta + add
        for c in range(chunks):
            rows = slice(c * HD, (c + 1) * HD)
            rounded = (sp[rows, :] * f_prompt).astype(BF)
            pt[keys + c * HD : keys + (c + 1) * HD, own] = rounded
            delta = delta + fold(rounded.astype(F32) * dpp[rows, :], jnp.sum)
        delta = jnp.sum(delta, axis=0, keepdims=True)
        for slot in range(4):
            dst[slot * HD : (slot + 1) * HD, own] = (
                (pr[quad, slot] * f_resp) * (dpr[quad, slot] - delta)
            ).astype(BF)
        for c in range(chunks):
            rows = slice(c * HD, (c + 1) * HD)
            dst[keys + c * HD : keys + (c + 1) * HD, own] = (
                (sp[rows, :] * f_prompt) * (dpp[rows, :] - delta)
            ).astype(BF)

    def full_quad(quad):
        full_half(quad, 0, pr_a, dpr_a, sp_a, dpp_a)
        full_half(quad, 1, pr_b, dpr_b, sp_b, dpp_b)

    def rows_of(ref, quad):
        part = ref[:, quad_cols(quad)]
        return jnp.concatenate([part[:, i * HD : (i + 1) * HD] for i in range(4)], axis=0)

    def add_keys(quad, lower, upper):
        second = lax.rem(quad, 2) == 1
        rows = slice(lower, upper)
        for acc, left, right in ((dv_acc, pt, do_ref), (dk_acc, dst, q_ref)):
            part = jnp.dot(left[rows, :], rows_of(right, quad), preferred_element_type=F32)
            acc[rows, :] = jnp.where(second, acc[rows, :], 0.0) + part

    def query_part(quad):
        g = lax.div(quad, 2)
        part = jnp.dot(kt[g], dst[...], preferred_element_type=F32)
        dq_ref[:, quad_cols(quad)] = jnp.concatenate(
            [(part[:, i * HD : (i + 1) * HD].T * SCALE).astype(BF) for i in range(4)], axis=1
        )

    def query_out(quad):
        cols = quad_cols(quad)
        return pltpu.make_async_copy(dq_ref.at[:, cols], dq_hbm.at[:, cols], s_out.at[quad])

    def emit(g):
        dk = dk_acc[keys:total, :] * SCALE
        dv = dv_acc[keys:total, :]
        pf[g] = jnp.concatenate(
            (dk.reshape(4 * nz, 8, HD), dv.reshape(4 * nz, 8, HD)), axis=1
        )
        for slot in range(4):
            rows = slice(slot * HD, (slot + 1) * HD)
            tf[g, slot, 0:HD, :] = dk_acc[rows, :] * SCALE
            tf[g, slot, HD : 2 * HD, :] = dv_acc[rows, :]

    def resp_quad(quad):
        resp_half(quad, 0, pr_a, dpr_a)
        resp_half(quad, 1, pr_b, dpr_b)

    make_bias()
    for g in range(HK):
        prompt_ready(g)
    resp_quad(0)
    resp_quad(1)
    full_quad(0)

    def both_step(quad, carry):
        add_keys(quad - 2, 0, total)
        query_part(quad - 2)
        resp_quad(quad)
        full_quad(quad - 1)
        query_out(quad - 2).start()

        @pl.when(lax.rem(quad, 2) == 1)
        def _():
            emit(lax.div(quad - 2, 2))

        return carry

    lax.fori_loop(2, quads, both_step, 0)
    add_keys(quads - 2, 0, total)
    query_part(quads - 2)
    full_quad(quads - 1)
    query_out(quads - 2).start()
    add_keys(quads - 1, 0, total)
    query_part(quads - 1)
    query_out(quads - 1).start()
    emit(HK - 1)
    for quad in range(quads):
        query_out(quad).wait()


def reduce_body(
    nz,
    pf,
    tf,
    drk_ref,
    drv_ref,
    dpk_ref,
    dpv_ref,
    ps,
    rc,
    xs,
    xf,
    rx,
    zs,
    zf,
    rz,
    ry,
    ys,
    tb,
    rp,
    ts,
    ra,
    rb,
    s_one,
    r_one,
):
    n = 4 * nz
    keys = 4 * HD
    npr = 32 * nz
    total = keys + npr
    me = lax.axis_index("seq")
    grp = lax.axis_index("grp")
    core = lax.rem(me, 2)
    x = lax.rem(lax.div(me, 2), 2)
    z = lax.div(me, 4)
    peer = me + 1 - 2 * core
    xpeer = me + 2 - 4 * x

    def zpeer(d):
        return lax.rem(me + 4 * d, n)

    def device(index):
        return (grp, index)

    def copy(src, dst, kind, g, to):
        return pltpu.make_async_remote_copy(
            src_ref=src,
            dst_ref=dst,
            send_sem=s_one.at[kind, g],
            recv_sem=r_one.at[kind, g],
            device_id=device(to),
            device_id_type=MESH,
        )

    barrier = pltpu.get_barrier_semaphore()

    def greet(to):
        pl.semaphore_signal(barrier, inc=1, device_id=device(to), device_id_type=MESH)

    greet(peer)
    greet(xpeer)
    greet(lax.rem(me + 2, n))
    greet(lax.rem(me + n - 2, n))
    greet(lax.rem(me + n + 6 * core - 3, n))

    for d in range(1, 5):
        greet(zpeer(d))
        greet(zpeer(nz - d))
    PC, PX, PZ, PY, PW, TP, TB, TA = range(8)
    half_blocks = 2 * nz
    for g in range(HK):
        ps[g] = pf[g, pl.ds((1 - core) * half_blocks, half_blocks)].astype(BF)
        for i in range(2):
            tb[g, i] = tf[g, 2 * i + 1].astype(BF)
    pl.semaphore_wait(barrier, 13)

    def pc_copy(g):
        return copy(ps.at[g], rc.at[g], PC, g, peer)

    def px_copy(g):
        return copy(xs.at[g], rx.at[g], PX, g, xpeer)

    def px_send(g):
        pc_copy(g).wait_recv()
        away = 1 - x
        xs[g] = (
            pf[g, pl.ds(core * half_blocks + away * nz, nz)]
            + rc[g, pl.ds(away * nz, nz)].astype(F32)
        ).astype(BF)
        xf[g] = (
            pf[g, pl.ds(core * half_blocks + x * nz, nz)] + rc[g, pl.ds(x * nz, nz)].astype(F32)
        )
        px_copy(g).start()

    def near(g, d, slot):
        return copy(zs.at[g, lax.rem(z + d, nz)], rz.at[g, slot], PZ, g, zpeer(d))

    def far(g, d, by, slot):
        return copy(zs.at[g, lax.rem(z + d, nz)], ry.at[g, slot], PY, g, zpeer(by))

    def relay(g, d, slot):
        return copy(ys.at[g, slot], rz.at[g, 6 + slot], PW, g, zpeer(d))

    def pz_send(g):
        px_copy(g).wait_recv()
        sums = xf[g] + rx[g].astype(F32)
        zf[g] = sums
        zs[g] = sums.astype(BF)
        for k in range(1, 5):
            far(g, nz - 4 - k, nz - k, k - 1).start()
        for k in range(1, 4):
            far(g, 4 + k, k, 3 + k).start()
        for k in range(1, 4):
            near(g, k, k - 1).start()
            near(g, nz - k, 2 + k).start()

    def far_all(g):
        return copy(zs.at[g, pl.ds(0, 7)], ry.at[g], PY, g, peer)

    def near_all(g):
        return copy(zs.at[g, pl.ds(0, 6)], rz.at[g, pl.ds(0, 6)], PZ, g, peer)

    def relay_all(g):
        return copy(ys.at[g], rz.at[g, pl.ds(6, 2)], PW, g, peer)

    def pw_send(g):
        far_all(g).wait_recv()
        below = zf[g, lax.rem(z + nz - 4, nz)] + jnp.sum(ry[g, 0:4].astype(F32), axis=0)
        above = zf[g, lax.rem(z + 4, nz)] + jnp.sum(ry[g, 4:7].astype(F32), axis=0)
        ys[g, 0] = below.astype(BF)
        ys[g, 1] = above.astype(BF)
        relay(g, nz - 4, 0).start()
        relay(g, 4, 1).start()

    def prompt_out(g):
        near_all(g).wait_recv()
        relay_all(g).wait_recv()
        sums = zf[g, z] + jnp.sum(rz[g].astype(F32), axis=0)
        cols = slice(g * HD, (g + 1) * HD)
        dpk_ref[:, cols] = sums[0:8]
        dpv_ref[:, cols] = sums[8:16]

    def tp_copy(g):
        return copy(tb.at[g, core], rp.at[g], TP, g, peer)

    def tb_copy(g):
        return copy(tb.at[g, 1 - core], rb.at[g], TB, g, lax.rem(me + n - 3 + 2 * core, n))

    def ta_copy(g):
        return copy(ts.at[g], ra.at[g], TA, g, lax.rem(me + n - 2, n))

    def ts_send(g):
        tp_copy(g).wait_recv()
        ts[g] = (tf[g, 2] + rp[g].astype(F32)).astype(BF)
        ta_copy(g).start()

    def resp_out(g):
        ta_copy(g).wait_recv()
        tb_copy(g).wait_recv()
        sums = tf[g, 0] + ra[g].astype(F32) + rb[g].astype(F32)
        cols = slice(g * HD, (g + 1) * HD)
        drk_ref[:, cols] = sums[0:HD]
        drv_ref[:, cols] = sums[HD : 2 * HD]

    for g in range(HK):
        pc_copy(g).start()
        tp_copy(g).start()
    for g in range(HK):
        px_send(g)
        ts_send(g)
        tb_copy(g).start()
    for g in range(HK):
        pz_send(g)
    for g in range(HK):
        pw_send(g)
    for g in range(HK):
        resp_out(g)
        prompt_out(g)
    for g in range(HK):
        for one in (pc_copy, px_copy, near_all, far_all, relay_all, tp_copy, tb_copy, ta_copy):
            one(g).wait_send()


def hand_over(*refs):
    sems = refs[8]
    copies = [pltpu.make_async_copy(refs[i], refs[4 + i], sems.at[i]) for i in range(4)]
    for one in copies:
        one.start()
    for one in copies:
        one.wait()


def on_device(queries, resp_key, resp_value, prompt_key, prompt_value, out_grad, segment):
    n = lax.axis_size("seq")
    nz = n // 4
    rows = queries.shape[0]
    npr = 32 * nz
    total = 4 * HD + npr
    quads = 2 * HK
    flat = HK * GROUP * HD
    vmem = pl.BlockSpec(memory_space=pltpu.VMEM)
    whole = pl.BlockSpec(memory_space=pl.ANY)
    shape = jax.ShapeDtypeStruct

    def space(*pieces):
        return [pltpu.VMEM(dims, kind) for dims, kind in pieces]

    def dma(*dims):
        return pltpu.SemaphoreType.DMA(dims)

    win, gat = pl.pallas_call(
        lambda *refs: gather_body(nz, *refs),
        out_shape=[
            shape((HK, 4, 2 * HD + 16, HD), BF),
            shape((2, 2, nz, HK, 16, HD), BF),
        ],
        in_specs=[vmem] * 5,
        out_specs=[vmem] * 2,
        scratch_shapes=[dma(HK, 3), dma(HK, 4), dma(1), dma(nz), dma(2, HK), dma(2, HK)],
        compiler_params=pltpu.CompilerParams(
            collective_id=0, has_side_effects=True, vmem_limit_bytes=32 * 1024 * 1024
        ),
        name="gather",
    )(resp_key, resp_value, prompt_key, prompt_value, segment.reshape(1, rows))
    dq, pf, tf = pl.pallas_call(
        lambda *refs: compute_body(nz, *refs),
        out_shape=[
            shape((rows, flat), BF),
            shape((HK, 4 * nz, 16, HD), F32),
            shape((HK, 4, 2 * HD, HD), F32),
        ],
        in_specs=[whole, whole, vmem, vmem],
        out_specs=[whole, vmem, vmem],
        scratch_shapes=space(
            ((rows, flat), BF),
            ((rows, flat), BF),
            ((rows, flat), BF),
            ((HD, flat), BF),
            ((HD, flat), BF),
            ((4, HD, HD), F32),
            ((quads, 4, HD, 2 * HD), F32),
            ((quads, 4, HD, 2 * HD), F32),
            ((quads, 4, HD, 2 * HD), F32),
            ((quads, 4, HD, 2 * HD), F32),
            ((quads, 2, 8, 2 * HD), F32),
            ((quads, 2, 8, 2 * HD), F32),
            ((npr, 2 * HD), F32),
            ((npr, 2 * HD), F32),
            ((npr, 2 * HD), F32),
            ((npr, 2 * HD), F32),
            ((HK, npr, HD), BF),
            ((HK, npr, HD), BF),
            ((HK, HD, total), BF),
            ((total, 4 * HD), BF),
            ((total, 4 * HD), BF),
            ((total, HD), F32),
            ((total, HD), F32),
        )
        + [dma(2), dma(quads)],
        compiler_params=pltpu.CompilerParams(vmem_limit_bytes=56 * 1024 * 1024),
        name="attention_backward",
    )(queries, out_grad, win, gat)
    results = pl.pallas_call(
        lambda *refs: reduce_body(nz, *refs),
        out_shape=[
            shape((rows, HK * HD), F32),
            shape((rows, HK * HD), F32),
            shape((8, HK * HD), F32),
            shape((8, HK * HD), F32),
        ],
        in_specs=[vmem] * 2,
        out_specs=[vmem] * 4,
        scratch_shapes=space(
            ((HK, 2 * nz, 16, HD), BF),
            ((HK, 2 * nz, 16, HD), BF),
            ((HK, nz, 16, HD), BF),
            ((HK, nz, 16, HD), F32),
            ((HK, nz, 16, HD), BF),
            ((HK, nz, 16, HD), BF),
            ((HK, nz, 16, HD), F32),
            ((HK, 8, 16, HD), BF),
            ((HK, 7, 16, HD), BF),
            ((HK, 2, 16, HD), BF),
            ((HK, 2, 2 * HD, HD), BF),
            ((HK, 2 * HD, HD), BF),
            ((HK, 2 * HD, HD), BF),
            ((HK, 2 * HD, HD), BF),
            ((HK, 2 * HD, HD), BF),
        )
        + [dma(8, HK), dma(8, HK)],
        compiler_params=pltpu.CompilerParams(
            collective_id=1, has_side_effects=True, vmem_limit_bytes=32 * 1024 * 1024
        ),
        name="reduce",
    )(pf, tf)
    handed = pl.pallas_call(
        hand_over,
        out_shape=[shape(r.shape, r.dtype) for r in results],
        in_specs=[vmem] * 4,
        out_specs=[whole] * 4,
        scratch_shapes=[dma(4)],
        name="hand_over",
    )(*results)
    return (dq, *handed)


def solution(mesh):
    spec = P(("grp", "seq"), None)
    return jax.shard_map(
        on_device,
        mesh=mesh,
        in_specs=(spec,) * 6 + (P(("grp", "seq")),),
        out_specs=(spec,) * 5,
        check_vma=False,
    )
```

```python
import jax
import jax.numpy as jnp
from jax import lax
from jax.experimental import pallas as pl
from jax.experimental.pallas import tpu as pltpu
from jax.sharding import PartitionSpec as P

MESH = pl.DeviceIdType.MESH
HD = 128
HK = 4
GROUP = 8
PAIRS = GROUP // 2
SCALE = HD ** (-0.5)
BF = jnp.bfloat16
F32 = jnp.float32


def body(
    nz,
    q_hbm,
    rk_hbm,
    rv_hbm,
    pk_hbm,
    pv_hbm,
    do_hbm,
    seg_hbm,
    dq_hbm,
    drk_ref,
    drv_ref,
    dpk_ref,
    dpv_ref,
    rk_ref,
    rv_ref,
    pk_ref,
    pv_ref,
    seg_ref,
    q_ref,
    do_ref,
    dq_ref,
    qt,
    dot,
    win,
    gat,
    bias,
    pr_a,
    pr_b,
    dpr_a,
    dpr_b,
    mr,
    lr,
    sp_a,
    sp_b,
    dpp_a,
    dpp_b,
    kp,
    vp,
    kt,
    pt,
    dst,
    dk_acc,
    dv_acc,
    ps,
    pf,
    rc,
    xs,
    xf,
    rx,
    zs,
    zf,
    rz,
    ry,
    ys,
    tb,
    tf,
    rp,
    ts,
    ra,
    rb,
    s_kv,
    r_kv,
    s_ring,
    r_ring,
    s_one,
    r_one,
    s_in,
    s_out,
):
    n = 4 * nz
    keys = 4 * HD
    npr = 32 * nz
    total = keys + npr
    quads = 2 * HK
    wide = 4 * HD
    me = lax.axis_index("seq")
    grp = lax.axis_index("grp")
    core = lax.rem(me, 2)
    x = lax.rem(lax.div(me, 2), 2)
    z = lax.div(me, 4)
    peer = me + 1 - 2 * core
    xpeer = me + 2 - 4 * x

    def zpeer(d):
        return lax.rem(me + 4 * d, n)

    def device(index):
        return (grp, index)

    GX, GC, PC, PX, PZ, PY, PW, TP, TB, TA = range(10)

    def copy(src, dst, kind, g, to):
        return pltpu.make_async_remote_copy(
            src_ref=src,
            dst_ref=dst,
            send_sem=s_one.at[kind, g],
            recv_sem=r_one.at[kind, g],
            device_id=device(to),
            device_id_type=MESH,
        )

    small = [
        pltpu.make_async_copy(source, target, s_in.at[2 + i])
        for i, (source, target) in enumerate(
            (
                (rk_hbm, rk_ref),
                (rv_hbm, rv_ref),
                (pk_hbm, pk_ref),
                (pv_hbm, pv_ref),
                (seg_hbm, seg_ref),
            )
        )
    ]
    q_in = pltpu.make_async_copy(q_hbm, q_ref, s_in.at[0])
    do_in = pltpu.make_async_copy(do_hbm, do_ref, s_in.at[1])
    for one in (*small, q_in, do_in):
        one.start()

    barrier = pltpu.get_barrier_semaphore()

    def greet(to):
        pl.semaphore_signal(barrier, inc=1, device_id=device(to), device_id_type=MESH)

    greet(peer)
    greet(xpeer)
    greet(lax.rem(me + 2, n))
    greet(lax.rem(me + n - 2, n))
    greet(lax.rem(me + n + 6 * core - 3, n))

    for d in range(1, 5):
        greet(zpeer(d))
        greet(zpeer(nz - d))
    for one in small:
        one.wait()

    labels = jnp.broadcast_to((seg_ref[...] + 1).astype(F32), (16, HD)).astype(BF)
    for g in range(HK):
        cols = slice(g * HD, (g + 1) * HD)
        win[g, 0, 0:HD, :] = rk_ref[:, cols]
        win[g, 0, HD : 2 * HD, :] = rv_ref[:, cols]
        win[g, 0, 2 * HD : 2 * HD + 16, :] = labels
        gat[core, x, z, g] = jnp.concatenate(
            (pk_ref[:, cols].astype(F32), pv_ref[:, cols].astype(F32)), axis=0
        ).astype(BF)
    pl.semaphore_wait(barrier, 13)

    def kv_copy(g, which, from_slot, to_slot, to):
        return pltpu.make_async_remote_copy(
            src_ref=win.at[g, from_slot],
            dst_ref=win.at[g, to_slot],
            send_sem=s_kv.at[g, which],
            recv_sem=r_kv.at[g, to_slot],
            device_id=device(to),
            device_id_type=MESH,
        )

    def kv_far(g):
        return kv_copy(g, 0, 0, 2, lax.rem(me + 2, n))

    def kv_side(g):
        return kv_copy(g, 1, 0, 1 + 2 * core, lax.rem(me + 1 + 2 * core, n))

    def kv_pass(g):
        return kv_copy(g, 2, 2, 3 - 2 * core, peer)

    def kv_forward(g):
        kv_far(g).wait_recv()
        kv_pass(g).start()

    def kv_ready(g):
        kv_copy(g, 1, 0, 1, peer).wait_recv()
        kv_copy(g, 1, 0, 3, peer).wait_recv()

    steps = nz // 4

    def ring_copy(owner, to, d):
        part = gat.at[core, x, owner]
        return pltpu.make_async_remote_copy(
            src_ref=part,
            dst_ref=part,
            send_sem=s_ring.at[0],
            recv_sem=r_ring.at[d],
            device_id=device(to),
            device_id_type=MESH,
        )

    def ring_wait(d):
        ring_copy(lax.rem(z + nz - d, nz), peer, d).wait_recv()

    def ring_step(k):
        if k > 1:
            ring_wait(2 * (k - 1))
            ring_wait(nz - 2 * (k - 1))
        up = lax.rem(z + nz - 2 * (k - 1), nz)
        down = lax.rem(z + 2 * (k - 1), nz)
        ring_copy(up, zpeer(2), 2 * k).start()
        if k < steps:
            ring_copy(down, zpeer(nz - 2), nz - 2 * k).start()
        ring_copy(up, zpeer(1), 2 * k - 1).start()
        ring_copy(down, zpeer(nz - 1), nz - 2 * k + 1).start()

    def gx_copy(g):
        part = gat.at[core, x, pl.ds(0, nz), g]
        return copy(part, part, GX, g, xpeer)

    def gc_copy(g):
        part = gat.at[core, pl.ds(0, 2), pl.ds(0, nz), g]
        return copy(part, part, GC, g, peer)

    def ring_end():
        for k in range(1, steps + 1):
            ring_wait(2 * k - 1)
            ring_wait(nz - 2 * k + 1)
        ring_wait(2 * steps)

    def gather_x(g):
        gx_copy(g).start()

    def gather_c(g):
        gx_copy(g).wait_recv()
        gc_copy(g).start()

    def kv_send(g):
        kv_far(g).start()
        kv_side(g).start()

    kv_send(0)
    ring_step(1)

    q_in.wait()
    do_in.wait()

    def flip(h, carry):
        for i in range(4):
            cols = pl.ds(pl.multiple_of((h * 4 + i) * HD, HD), HD)
            qt[:, cols] = q_ref[:, cols].T
            dot[:, cols] = do_ref[:, cols].T
        return carry

    lax.fori_loop(0, HK * GROUP // 8, flip, 0)
    kv_send(1)
    ring_step(2)
    lax.fori_loop(HK * GROUP // 8, HK * GROUP // 4, flip, 0)
    kv_forward(0)
    kv_send(2)
    ring_step(3)

    def make_bias():
        mine = jnp.broadcast_to(win[0, 0, 2 * HD : 2 * HD + 16, :].astype(F32)[0:1], (HD, HD))
        row = lax.broadcasted_iota(jnp.int32, (HD, HD), 1)
        col = lax.broadcasted_iota(jnp.int32, (HD, HD), 0)
        for slot in range(4):
            theirs = jnp.broadcast_to(
                win[0, slot, 2 * HD : 2 * HD + 16, :].astype(F32)[0:1], (HD, HD)
            ).T
            seen = mine == theirs
            if slot == 0:
                seen = seen & (col <= row)
            else:
                seen = seen & (jnp.broadcast_to(me, (HD, HD)) >= slot)
            bias[slot] = jnp.where(seen, 0.0, -jnp.inf)

    def fold(value, op):
        return op(value.reshape(value.shape[0] // 8, 8, value.shape[1]), axis=0)

    def half_cols(quad, half):
        return pl.ds(pl.multiple_of(quad * wide + half * 2 * HD, 2 * HD), 2 * HD)

    def quad_cols(quad):
        return pl.ds(pl.multiple_of(quad * wide, wide), wide)

    def resp_half(quad, half, pr, dpr):
        g = lax.div(quad, 2)
        cols = half_cols(quad, half)
        k4 = win[g, :, 0:HD, :].reshape(keys, HD)
        v4 = win[g, :, HD : 2 * HD, :].reshape(keys, HD)
        scores = jnp.dot(k4, qt[:, cols], preferred_element_type=F32)
        high = None
        for slot in range(4):
            mask = bias[slot]
            part = scores[slot * HD : (slot + 1) * HD] + jnp.concatenate((mask, mask), axis=1)
            pr[quad, slot] = part
            top = fold(part, jnp.max)
            high = top if high is None else jnp.maximum(high, top)
        high = jnp.max(high, axis=0, keepdims=True)
        dpr[quad] = jnp.dot(v4, dot[:, cols], preferred_element_type=F32).reshape(4, HD, 2 * HD)
        low = None
        for slot in range(4):
            part = jnp.exp((pr[quad, slot] - high) * SCALE)
            pr[quad, slot] = part
            add = fold(part, jnp.sum)
            low = add if low is None else low + add
        mr[quad, half] = jnp.broadcast_to(high, (8, 2 * HD))
        lr[quad, half] = jnp.broadcast_to(jnp.sum(low, axis=0, keepdims=True), (8, 2 * HD))

    def prompt_ready(g):
        gc_copy(g).wait_recv()
        all_rows = gat[:, :, :, g].reshape(4 * nz, 16, HD).astype(F32)
        kp[g] = all_rows[:, 0:8].reshape(npr, HD).astype(BF)
        vp[g] = all_rows[:, 8:16].reshape(npr, HD).astype(BF)
        for slot in range(4):
            kt[g, :, slot * HD : (slot + 1) * HD] = win[g, slot, 0:HD, :].T
        for lower in range(0, npr, HD):
            kt[g, :, keys + lower : keys + lower + HD] = kp[g, lower : lower + HD, :].T

    chunks = npr // HD

    def full_half(quad, half, pr, dpr, sp, dpp):
        g = lax.div(quad, 2)
        cols = half_cols(quad, half)
        own = slice(half * 2 * HD, (half + 1) * 2 * HD)
        scores = jnp.dot(kp[g], qt[:, cols], preferred_element_type=F32)
        sp[...] = scores
        high = jnp.maximum(mr[quad, half], fold(scores, jnp.max))
        dpp[...] = jnp.dot(vp[g], dot[:, cols], preferred_element_type=F32)
        old = mr[quad, half][0:1]
        high = jnp.max(high, axis=0, keepdims=True)
        low = None
        for c in range(chunks):
            rows = slice(c * HD, (c + 1) * HD)
            part = jnp.exp((sp[rows, :] - high) * SCALE)
            sp[rows, :] = part
            add = fold(part, jnp.sum)
            low = add if low is None else low + add
        shrink = jnp.exp((old - high) * SCALE)
        sums = jnp.sum(low, axis=0, keepdims=True) + lr[quad, half][0:1] * shrink
        f_prompt = 1.0 / sums
        f_resp = shrink * f_prompt
        delta = None
        for slot in range(4):
            rounded = (pr[quad, slot] * f_resp).astype(BF)
            pt[slot * HD : (slot + 1) * HD, own] = rounded
            add = fold(rounded.astype(F32) * dpr[quad, slot], jnp.sum)
            delta = add if delta is None else delta + add
        for c in range(chunks):
            rows = slice(c * HD, (c + 1) * HD)
            rounded = (sp[rows, :] * f_prompt).astype(BF)
            pt[keys + c * HD : keys + (c + 1) * HD, own] = rounded
            delta = delta + fold(rounded.astype(F32) * dpp[rows, :], jnp.sum)
        delta = jnp.sum(delta, axis=0, keepdims=True)
        for slot in range(4):
            dst[quad, slot * HD : (slot + 1) * HD, own] = (
                (pr[quad, slot] * f_resp) * (dpr[quad, slot] - delta)
            ).astype(BF)
        for c in range(chunks):
            rows = slice(c * HD, (c + 1) * HD)
            dst[quad, keys + c * HD : keys + (c + 1) * HD, own] = (
                (sp[rows, :] * f_prompt) * (dpp[rows, :] - delta)
            ).astype(BF)

    def full_quad(quad):
        full_half(quad, 0, pr_a, dpr_a, sp_a, dpp_a)
        full_half(quad, 1, pr_b, dpr_b, sp_b, dpp_b)

    def rows_of(ref, quad):
        part = ref[:, quad_cols(quad)]
        return jnp.concatenate([part[:, i * HD : (i + 1) * HD] for i in range(4)], axis=0)

    def add_keys(quad, lower, upper):
        second = lax.rem(quad, 2) == 1
        rows = slice(lower, upper)
        for acc, left, right in ((dv_acc, pt, do_ref), (dk_acc, dst.at[quad], q_ref)):
            part = jnp.dot(left[rows, :], rows_of(right, quad), preferred_element_type=F32)
            acc[rows, :] = jnp.where(second, acc[rows, :], 0.0) + part

    def query_part(quad):
        g = lax.div(quad, 2)
        part = jnp.dot(kt[g], dst[quad], preferred_element_type=F32)
        dq_ref[:, quad_cols(quad)] = jnp.concatenate(
            [(part[:, i * HD : (i + 1) * HD].T * SCALE).astype(BF) for i in range(4)], axis=1
        )

    def query_out(quad):
        cols = quad_cols(quad)
        return pltpu.make_async_copy(dq_ref.at[:, cols], dq_hbm.at[:, cols], s_out.at[quad])

    def emit_prompt(g):
        dk = dk_acc[keys:total, :] * SCALE
        dv = dv_acc[keys:total, :]
        both = jnp.concatenate(
            (dk.reshape(4 * nz, 8, HD), dv.reshape(4 * nz, 8, HD)), axis=1
        )
        pf[g] = both
        ps[g] = both.astype(BF)
        pc_copy(g).start()

    def emit_resp(g):
        for slot in range(4):
            rows = slice(slot * HD, (slot + 1) * HD)
            dk = dk_acc[rows, :] * SCALE
            dv = dv_acc[rows, :]
            if slot in (0, 2):
                tf[g, slot // 2, 0:HD, :] = dk
                tf[g, slot // 2, HD : 2 * HD, :] = dv
            else:
                tb[g, slot // 2, 0:HD, :] = dk.astype(BF)
                tb[g, slot // 2, HD : 2 * HD, :] = dv.astype(BF)
        tp_copy(g).start()
        tb_copy(g).start()

    half_blocks = 2 * nz

    def pc_copy(g):
        return copy(
            ps.at[g, pl.ds((1 - core) * half_blocks, half_blocks)], rc.at[g], PC, g, peer
        )

    def px_copy(g):
        return copy(xs.at[g], rx.at[g], PX, g, xpeer)

    def px_send(g):
        pc_copy(g).wait_recv()
        away = 1 - x
        xs[g] = (
            pf[g, pl.ds(core * half_blocks + away * nz, nz)]
            + rc[g, pl.ds(away * nz, nz)].astype(F32)
        ).astype(BF)
        xf[g] = (
            pf[g, pl.ds(core * half_blocks + x * nz, nz)] + rc[g, pl.ds(x * nz, nz)].astype(F32)
        )
        px_copy(g).start()

    def near(g, d, slot):
        return copy(zs.at[g, lax.rem(z + d, nz)], rz.at[g, slot], PZ, g, zpeer(d))

    def far(g, d, by, slot):
        return copy(zs.at[g, lax.rem(z + d, nz)], ry.at[g, slot], PY, g, zpeer(by))

    def relay(g, d, slot):
        return copy(ys.at[g, slot], rz.at[g, 6 + slot], PW, g, zpeer(d))

    def pz_send(g):
        px_copy(g).wait_recv()
        sums = xf[g] + rx[g].astype(F32)
        zf[g] = sums
        zs[g] = sums.astype(BF)
        for k in range(1, 5):
            far(g, nz - 4 - k, nz - k, k - 1).start()
        for k in range(1, 4):
            far(g, 4 + k, k, 3 + k).start()
        for k in range(1, 4):
            near(g, k, k - 1).start()
            near(g, nz - k, 2 + k).start()

    def far_all(g):
        return copy(zs.at[g, pl.ds(0, 7)], ry.at[g], PY, g, peer)

    def near_all(g):
        return copy(zs.at[g, pl.ds(0, 6)], rz.at[g, pl.ds(0, 6)], PZ, g, peer)

    def relay_all(g):
        return copy(ys.at[g], rz.at[g, pl.ds(6, 2)], PW, g, peer)

    def pw_send(g):
        far_all(g).wait_recv()
        below = zf[g, lax.rem(z + nz - 4, nz)] + jnp.sum(ry[g, 0:4].astype(F32), axis=0)
        above = zf[g, lax.rem(z + 4, nz)] + jnp.sum(ry[g, 4:7].astype(F32), axis=0)
        ys[g, 0] = below.astype(BF)
        ys[g, 1] = above.astype(BF)
        relay(g, nz - 4, 0).start()
        relay(g, 4, 1).start()

    def prompt_out(g):
        near_all(g).wait_recv()
        relay_all(g).wait_recv()
        sums = zf[g, z] + jnp.sum(rz[g].astype(F32), axis=0)
        cols = slice(g * HD, (g + 1) * HD)
        dpk_ref[:, cols] = sums[0:8]
        dpv_ref[:, cols] = sums[8:16]

    def tp_copy(g):
        return copy(tb.at[g, core], rp.at[g], TP, g, peer)

    def tb_copy(g):
        return copy(tb.at[g, 1 - core], rb.at[g], TB, g, lax.rem(me + n - 3 + 2 * core, n))

    def ta_copy(g):
        return copy(ts.at[g], ra.at[g], TA, g, lax.rem(me + n - 2, n))

    def ts_send(g):
        tp_copy(g).wait_recv()
        ts[g] = (tf[g, 1] + rp[g].astype(F32)).astype(BF)
        ta_copy(g).start()

    def resp_out(g):
        ta_copy(g).wait_recv()
        tb_copy(g).wait_recv()
        sums = tf[g, 0] + ra[g].astype(F32) + rb[g].astype(F32)
        cols = slice(g * HD, (g + 1) * HD)
        drk_ref[:, cols] = sums[0:HD]
        drv_ref[:, cols] = sums[HD : 2 * HD]

    def when(flag, *calls):
        @pl.when(flag)
        def _():
            for call, g in calls:
                call(g)

    def resp_quad(quad):
        resp_half(quad, 0, pr_a, dpr_a)
        resp_half(quad, 1, pr_b, dpr_b)

    kv_ready(0)
    make_bias()

    def resp_step(quad, carry):
        when(quad == 2, (kv_ready, 1))
        resp_quad(quad)
        when(quad == 0, (ring_step, 4), (kv_forward, 1), (kv_send, 3))

        @pl.when(quad == 1)
        def _():
            ring_end()
            for g in range(HK):
                gather_x(g)

        when(quad == 2, (kv_forward, 2))
        when(quad == 3, (gather_c, 0))
        return carry

    lax.fori_loop(0, 4, resp_step, 0)
    kv_ready(2)
    prompt_ready(0)
    resp_quad(4)
    full_quad(0)
    gather_c(1)

    def both_step(quad, carry):
        when(quad == 6, (kv_ready, 3), (prompt_ready, 1))
        add_keys(quad - 5, 0, total)
        resp_quad(quad)
        full_quad(quad - 4)
        when(quad == 5, (kv_forward, 3))
        when(quad == 6, (emit_prompt, 0), (emit_resp, 0), (gather_c, 2))
        when(quad == 7, (gather_c, 3), (px_send, 0), (ts_send, 0))
        return carry

    lax.fori_loop(5, quads, both_step, 0)

    def full_step(quad, carry):
        g = lax.div(quad, 2)
        first = lax.rem(quad, 2) == 0
        when(first, (prompt_ready, g))
        add_keys(quad - 1, 0, total)
        full_quad(quad)
        when(first, (emit_prompt, g - 1), (emit_resp, g - 1), (pz_send, g - 2))
        when(~first, (px_send, g - 1), (ts_send, g - 1), (pw_send, g - 2))
        return carry

    lax.fori_loop(4, quads, full_step, 0)

    def query(*which):
        for quad in which:
            query_part(quad)
            query_out(quad).start()

    last = HK - 1
    add_keys(quads - 1, keys, total)
    emit_prompt(last)
    add_keys(quads - 1, 0, keys)
    emit_resp(last)
    pz_send(last - 1)
    query(0, 1, 2)
    px_send(last)
    ts_send(last)
    query(3, 4)
    pw_send(last - 1)
    query(5)
    pz_send(last)
    query(6, 7)
    for g in range(last):
        prompt_out(g)
        resp_out(g)
    pw_send(last)
    resp_out(last)
    prompt_out(last)

    sent = gat.at[0, 0, pl.ds(0, nz - 1)]
    pltpu.make_async_remote_copy(
        src_ref=sent,
        dst_ref=sent,
        send_sem=s_ring.at[0],
        recv_sem=r_ring.at[0],
        device_id=device(peer),
        device_id_type=MESH,
    ).wait_send()
    for g in range(HK):
        kv_far(g).wait_send()
        kv_side(g).wait_send()
        kv_pass(g).wait_send()
        gx_copy(g).wait_send()
        gc_copy(g).wait_send()
        pc_copy(g).wait_send()
        px_copy(g).wait_send()
        near_all(g).wait_send()
        far_all(g).wait_send()
        relay_all(g).wait_send()
        tp_copy(g).wait_send()
        tb_copy(g).wait_send()
        ta_copy(g).wait_send()
    for quad in range(quads):
        query_out(quad).wait()


def hand_over(*refs):
    sems = refs[10]
    copies = [
        pltpu.make_async_copy(refs[i], refs[5 + i], sems.at[i]) for i in range(5)
    ]
    for one in copies:
        one.start()
    for one in copies:
        one.wait()


def on_device(queries, resp_key, resp_value, prompt_key, prompt_value, out_grad, segment):
    n = lax.axis_size("seq")
    nz = n // 4
    rows = queries.shape[0]
    npr = 32 * nz
    total = 4 * HD + npr
    quads = 2 * HK
    vmem = pl.BlockSpec(memory_space=pltpu.VMEM)
    whole = pl.BlockSpec(memory_space=pl.ANY)
    flat = HK * GROUP * HD
    scratch = [
        ((rows, HK * HD), BF),
        ((rows, HK * HD), BF),
        ((8, HK * HD), BF),
        ((8, HK * HD), BF),
        ((1, rows), jnp.int32),
        ((rows, flat), BF),
        ((rows, flat), BF),
        ((rows, flat), BF),
        ((HD, flat), BF),
        ((HD, flat), BF),
        ((HK, 4, 2 * HD + 16, HD), BF),
        ((2, 2, nz, HK, 16, HD), BF),
        ((4, HD, HD), F32),
        ((quads, 4, HD, 2 * HD), F32),
        ((quads, 4, HD, 2 * HD), F32),
        ((quads, 4, HD, 2 * HD), F32),
        ((quads, 4, HD, 2 * HD), F32),
        ((quads, 2, 8, 2 * HD), F32),
        ((quads, 2, 8, 2 * HD), F32),
        ((npr, 2 * HD), F32),
        ((npr, 2 * HD), F32),
        ((npr, 2 * HD), F32),
        ((npr, 2 * HD), F32),
        ((HK, npr, HD), BF),
        ((HK, npr, HD), BF),
        ((HK, HD, total), BF),
        ((total, 4 * HD), BF),
        ((quads, total, 4 * HD), BF),
        ((total, HD), F32),
        ((total, HD), F32),
        ((HK, 4 * nz, 16, HD), BF),
        ((HK, 4 * nz, 16, HD), F32),
        ((HK, 2 * nz, 16, HD), BF),
        ((HK, nz, 16, HD), BF),
        ((HK, nz, 16, HD), F32),
        ((HK, nz, 16, HD), BF),
        ((HK, nz, 16, HD), BF),
        ((HK, nz, 16, HD), F32),
        ((HK, 8, 16, HD), BF),
        ((HK, 7, 16, HD), BF),
        ((HK, 2, 16, HD), BF),
        ((HK, 2, 2 * HD, HD), BF),
        ((HK, 2, 2 * HD, HD), F32),
        ((HK, 2 * HD, HD), BF),
        ((HK, 2 * HD, HD), BF),
        ((HK, 2 * HD, HD), BF),
        ((HK, 2 * HD, HD), BF),
    ]
    shapes = [
        jax.ShapeDtypeStruct((rows, flat), BF),
        jax.ShapeDtypeStruct((rows, HK * HD), F32),
        jax.ShapeDtypeStruct((rows, HK * HD), F32),
        jax.ShapeDtypeStruct((8, HK * HD), F32),
        jax.ShapeDtypeStruct((8, HK * HD), F32),
    ]
    results = pl.pallas_call(
        lambda *refs: body(nz, *refs),
        out_shape=shapes,
        in_specs=[whole] * 7,
        out_specs=[whole] + [vmem] * 4,
        scratch_shapes=[pltpu.VMEM(shape, kind) for shape, kind in scratch]
        + [
            pltpu.SemaphoreType.DMA((HK, 3)),
            pltpu.SemaphoreType.DMA((HK, 4)),
            pltpu.SemaphoreType.DMA((1,)),
            pltpu.SemaphoreType.DMA((nz,)),
            pltpu.SemaphoreType.DMA((10, HK)),
            pltpu.SemaphoreType.DMA((10, HK)),
            pltpu.SemaphoreType.DMA((7,)),
            pltpu.SemaphoreType.DMA((quads,)),
        ],
        compiler_params=pltpu.CompilerParams(
            collective_id=0, has_side_effects=True, vmem_limit_bytes=60 * 1024 * 1024
        ),
        cost_estimate=pl.CostEstimate(
            flops=6 * 10**9, bytes_accessed=6 * 10**6, transcendentals=4 * 10**6
        ),
        name="attention_backward",
    )(
        queries,
        resp_key,
        resp_value,
        prompt_key,
        prompt_value,
        out_grad,
        segment.reshape(1, rows),
    )
    return tuple(
        pl.pallas_call(
            hand_over,
            out_shape=shapes,
            in_specs=[vmem] * 5,
            out_specs=[whole] * 5,
            scratch_shapes=[pltpu.SemaphoreType.DMA((5,))],
            cost_estimate=pl.CostEstimate(
                flops=0, bytes_accessed=3 * 10**6, transcendentals=0
            ),
            name="hand_over",
        )(*results)
    )


def solution(mesh):
    spec = P(("grp", "seq"), None)
    return jax.shard_map(
        on_device,
        mesh=mesh,
        in_specs=(spec,) * 6 + (P(("grp", "seq")),),
        out_specs=(spec,) * 5,
        check_vma=False,
    )
```

```python
import jax
import jax.numpy as jnp
from jax import lax
from jax.experimental import pallas as pl
from jax.experimental.pallas import tpu as pltpu
from jax.sharding import PartitionSpec as P

MESH = pl.DeviceIdType.MESH
HD = 128
HK = 4
GROUP = 8
PAIRS = GROUP // 2
SCALE = HD ** (-0.5)
BF = jnp.bfloat16
F32 = jnp.float32


def body(
    nz,
    q_hbm,
    rk_hbm,
    rv_hbm,
    pk_hbm,
    pv_hbm,
    do_hbm,
    seg_hbm,
    dq_hbm,
    drk_ref,
    drv_ref,
    dpk_ref,
    dpv_ref,
    rk_ref,
    rv_ref,
    pk_ref,
    pv_ref,
    seg_ref,
    q_ref,
    do_ref,
    dq_ref,
    qt,
    dot,
    win,
    gat,
    bias,
    pr_a,
    pr_b,
    dpr_a,
    dpr_b,
    mr,
    lr,
    sp_a,
    sp_b,
    dpp_a,
    dpp_b,
    kp,
    vp,
    kt,
    pt,
    dst,
    dk_acc,
    dv_acc,
    ps,
    pf,
    rc,
    xs,
    xf,
    rx,
    zs,
    zf,
    rz,
    ry,
    ys,
    tb,
    tf,
    rp,
    ts,
    ra,
    rb,
    s_kv,
    r_kv,
    s_ring,
    r_ring,
    s_one,
    r_one,
    s_in,
    s_out,
):
    n = 4 * nz
    keys = 4 * HD
    npr = 32 * nz
    total = keys + npr
    quads = 2 * HK
    wide = 4 * HD
    me = lax.axis_index("seq")
    grp = lax.axis_index("grp")
    core = lax.rem(me, 2)
    x = lax.rem(lax.div(me, 2), 2)
    z = lax.div(me, 4)
    peer = me + 1 - 2 * core
    xpeer = me + 2 - 4 * x

    def zpeer(d):
        return lax.rem(me + 4 * d, n)

    def device(index):
        return (grp, index)

    GX, GC, PC, PX, PZ, PY, PW, TP, TB, TA, GZ = range(11)

    def copy(src, dst, kind, g, to):
        return pltpu.make_async_remote_copy(
            src_ref=src,
            dst_ref=dst,
            send_sem=s_one.at[kind, g],
            recv_sem=r_one.at[kind, g],
            device_id=device(to),
            device_id_type=MESH,
        )

    small = [
        pltpu.make_async_copy(source, target, s_in.at[2 + i])
        for i, (source, target) in enumerate(
            (
                (rk_hbm, rk_ref),
                (rv_hbm, rv_ref),
                (pk_hbm, pk_ref),
                (pv_hbm, pv_ref),
                (seg_hbm, seg_ref),
            )
        )
    ]
    q_in = pltpu.make_async_copy(q_hbm, q_ref, s_in.at[0])
    do_in = pltpu.make_async_copy(do_hbm, do_ref, s_in.at[1])
    for one in (*small, q_in, do_in):
        one.start()

    barrier = pltpu.get_barrier_semaphore()

    def greet(to):
        pl.semaphore_signal(barrier, inc=1, device_id=device(to), device_id_type=MESH)

    greet(peer)
    greet(xpeer)
    greet(lax.rem(me + 2, n))
    greet(lax.rem(me + n - 2, n))
    greet(lax.rem(me + n + 6 * core - 3, n))

    for d in range(1, nz):
        greet(zpeer(d))
    for one in small:
        one.wait()

    labels = jnp.broadcast_to((seg_ref[...] + 1).astype(F32), (16, HD)).astype(BF)
    for g in range(HK):
        cols = slice(g * HD, (g + 1) * HD)
        win[g, 0, 0:HD, :] = rk_ref[:, cols]
        win[g, 0, HD : 2 * HD, :] = rv_ref[:, cols]
        win[g, 0, 2 * HD : 2 * HD + 16, :] = labels
        gat[core, x, z, g] = jnp.concatenate(
            (pk_ref[:, cols].astype(F32), pv_ref[:, cols].astype(F32)), axis=0
        ).astype(BF)
    pl.semaphore_wait(barrier, 5 + nz - 1)

    def kv_copy(g, which, from_slot, to_slot, to):
        return pltpu.make_async_remote_copy(
            src_ref=win.at[g, from_slot],
            dst_ref=win.at[g, to_slot],
            send_sem=s_kv.at[g, which],
            recv_sem=r_kv.at[g, to_slot],
            device_id=device(to),
            device_id_type=MESH,
        )

    def kv_far(g):
        return kv_copy(g, 0, 0, 2, lax.rem(me + 2, n))

    def kv_side(g):
        return kv_copy(g, 1, 0, 1 + 2 * core, lax.rem(me + 1 + 2 * core, n))

    def kv_pass(g):
        return kv_copy(g, 2, 2, 3 - 2 * core, peer)

    def kv_forward(g):
        kv_far(g).wait_recv()
        kv_pass(g).start()

    def kv_ready(g):
        kv_copy(g, 1, 0, 1, peer).wait_recv()
        kv_copy(g, 1, 0, 3, peer).wait_recv()

    steps = nz // 4

    def ring_copy(owner, to, d):
        part = gat.at[core, x, owner, pl.ds(1, HK - 1)]
        return pltpu.make_async_remote_copy(
            src_ref=part,
            dst_ref=part,
            send_sem=s_ring.at[0],
            recv_sem=r_ring.at[d],
            device_id=device(to),
            device_id_type=MESH,
        )

    def ring_wait(d):
        ring_copy(lax.rem(z + nz - d, nz), peer, d).wait_recv()

    def ring_step(k):
        if k > 1:
            ring_wait(2 * (k - 1))
            ring_wait(nz - 2 * (k - 1))
        up = lax.rem(z + nz - 2 * (k - 1), nz)
        down = lax.rem(z + 2 * (k - 1), nz)
        ring_copy(up, zpeer(2), 2 * k).start()
        if k < steps:
            ring_copy(down, zpeer(nz - 2), nz - 2 * k).start()
        ring_copy(up, zpeer(1), 2 * k - 1).start()
        ring_copy(down, zpeer(nz - 1), nz - 2 * k + 1).start()

    def gz_copy(d):
        part = gat.at[core, x, z, 0]
        return copy(part, part, GZ, 0, zpeer(d))

    def gz_all():
        part = gat.at[core, x, pl.ds(0, nz - 1), 0]
        return copy(part, part, GZ, 0, peer)

    def gx_copy(g):
        part = gat.at[core, x, pl.ds(0, nz), g]
        return copy(part, part, GX, g, xpeer)

    def gc_copy(g):
        part = gat.at[core, pl.ds(0, 2), pl.ds(0, nz), g]
        return copy(part, part, GC, g, peer)

    def ring_end():
        for k in range(1, steps + 1):
            ring_wait(2 * k - 1)
            ring_wait(nz - 2 * k + 1)
        ring_wait(2 * steps)

    def gather_x(g):
        gx_copy(g).start()

    def gather_c(g):
        gx_copy(g).wait_recv()
        gc_copy(g).start()

    def kv_send(g):
        kv_far(g).start()
        kv_side(g).start()

    kv_send(0)
    for d in range(1, nz // 2):
        gz_copy(nz // 2 - d).start()
        gz_copy(nz // 2 + d).start()
    gz_copy(nz // 2).start()
    ring_step(1)

    q_in.wait()
    do_in.wait()

    def flip(h, carry):
        for i in range(4):
            cols = pl.ds(pl.multiple_of((h * 4 + i) * HD, HD), HD)
            qt[:, cols] = q_ref[:, cols].T
            dot[:, cols] = do_ref[:, cols].T
        return carry

    lax.fori_loop(0, HK * GROUP // 8, flip, 0)
    kv_forward(0)
    kv_send(1)
    ring_step(2)
    lax.fori_loop(HK * GROUP // 8, HK * GROUP // 4, flip, 0)
    gz_all().wait_recv()
    gx_copy(0).start()

    def make_bias():
        mine = jnp.broadcast_to(win[0, 0, 2 * HD : 2 * HD + 16, :].astype(F32)[0:1], (HD, HD))
        row = lax.broadcasted_iota(jnp.int32, (HD, HD), 1)
        col = lax.broadcasted_iota(jnp.int32, (HD, HD), 0)
        for slot in range(4):
            theirs = jnp.broadcast_to(
                win[0, slot, 2 * HD : 2 * HD + 16, :].astype(F32)[0:1], (HD, HD)
            ).T
            seen = mine == theirs
            if slot == 0:
                seen = seen & (col <= row)
            else:
                seen = seen & (jnp.broadcast_to(me, (HD, HD)) >= slot)
            bias[slot] = jnp.where(seen, 0.0, -jnp.inf)

    def fold(value, op):
        return op(value.reshape(value.shape[0] // 8, 8, value.shape[1]), axis=0)

    def half_cols(quad, half):
        return pl.ds(pl.multiple_of(quad * wide + half * 2 * HD, 2 * HD), 2 * HD)

    def quad_cols(quad):
        return pl.ds(pl.multiple_of(quad * wide, wide), wide)

    def resp_half(quad, half, pr, dpr):
        g = lax.div(quad, 2)
        cols = half_cols(quad, half)
        k4 = win[g, :, 0:HD, :].reshape(keys, HD)
        v4 = win[g, :, HD : 2 * HD, :].reshape(keys, HD)
        scores = jnp.dot(k4, qt[:, cols], preferred_element_type=F32)
        high = None
        for slot in range(4):
            mask = bias[slot]
            part = scores[slot * HD : (slot + 1) * HD] + jnp.concatenate((mask, mask), axis=1)
            pr[quad, slot] = part
            top = fold(part, jnp.max)
            high = top if high is None else jnp.maximum(high, top)
        high = jnp.max(high, axis=0, keepdims=True)
        dpr[quad] = jnp.dot(v4, dot[:, cols], preferred_element_type=F32).reshape(4, HD, 2 * HD)
        low = None
        for slot in range(4):
            part = jnp.exp((pr[quad, slot] - high) * SCALE)
            pr[quad, slot] = part
            add = fold(part, jnp.sum)
            low = add if low is None else low + add
        mr[quad, half] = jnp.broadcast_to(high, (8, 2 * HD))
        lr[quad, half] = jnp.broadcast_to(jnp.sum(low, axis=0, keepdims=True), (8, 2 * HD))

    def prompt_ready(g):
        gc_copy(g).wait_recv()
        all_rows = gat[:, :, :, g].reshape(4 * nz, 16, HD).astype(F32)
        kp[g] = all_rows[:, 0:8].reshape(npr, HD).astype(BF)
        vp[g] = all_rows[:, 8:16].reshape(npr, HD).astype(BF)
        for slot in range(4):
            kt[g, :, slot * HD : (slot + 1) * HD] = win[g, slot, 0:HD, :].T
        for lower in range(0, npr, HD):
            kt[g, :, keys + lower : keys + lower + HD] = kp[g, lower : lower + HD, :].T

    chunks = npr // HD

    def full_half(quad, half, pr, dpr, sp, dpp):
        g = lax.div(quad, 2)
        cols = half_cols(quad, half)
        own = slice(half * 2 * HD, (half + 1) * 2 * HD)
        scores = jnp.dot(kp[g], qt[:, cols], preferred_element_type=F32)
        sp[...] = scores
        high = jnp.maximum(mr[quad, half], fold(scores, jnp.max))
        dpp[...] = jnp.dot(vp[g], dot[:, cols], preferred_element_type=F32)
        old = mr[quad, half][0:1]
        high = jnp.max(high, axis=0, keepdims=True)
        low = None
        for c in range(chunks):
            rows = slice(c * HD, (c + 1) * HD)
            part = jnp.exp((sp[rows, :] - high) * SCALE)
            sp[rows, :] = part
            add = fold(part, jnp.sum)
            low = add if low is None else low + add
        shrink = jnp.exp((old - high) * SCALE)
        sums = jnp.sum(low, axis=0, keepdims=True) + lr[quad, half][0:1] * shrink
        f_prompt = 1.0 / sums
        f_resp = shrink * f_prompt
        delta = None
        for slot in range(4):
            rounded = (pr[quad, slot] * f_resp).astype(BF)
            pt[slot * HD : (slot + 1) * HD, own] = rounded
            add = fold(rounded.astype(F32) * dpr[quad, slot], jnp.sum)
            delta = add if delta is None else delta + add
        for c in range(chunks):
            rows = slice(c * HD, (c + 1) * HD)
            rounded = (sp[rows, :] * f_prompt).astype(BF)
            pt[keys + c * HD : keys + (c + 1) * HD, own] = rounded
            delta = delta + fold(rounded.astype(F32) * dpp[rows, :], jnp.sum)
        delta = jnp.sum(delta, axis=0, keepdims=True)
        for slot in range(4):
            dst[quad, slot * HD : (slot + 1) * HD, own] = (
                (pr[quad, slot] * f_resp) * (dpr[quad, slot] - delta)
            ).astype(BF)
        for c in range(chunks):
            rows = slice(c * HD, (c + 1) * HD)
            dst[quad, keys + c * HD : keys + (c + 1) * HD, own] = (
                (sp[rows, :] * f_prompt) * (dpp[rows, :] - delta)
            ).astype(BF)

    def full_quad(quad):
        full_half(quad, 0, pr_a, dpr_a, sp_a, dpp_a)
        full_half(quad, 1, pr_b, dpr_b, sp_b, dpp_b)

    def rows_of(ref, quad):
        part = ref[:, quad_cols(quad)]
        return jnp.concatenate([part[:, i * HD : (i + 1) * HD] for i in range(4)], axis=0)

    def add_keys(quad, lower, upper):
        second = lax.rem(quad, 2) == 1
        rows = slice(lower, upper)
        for acc, left, right in ((dv_acc, pt, do_ref), (dk_acc, dst.at[quad], q_ref)):
            part = jnp.dot(left[rows, :], rows_of(right, quad), preferred_element_type=F32)
            acc[rows, :] = jnp.where(second, acc[rows, :], 0.0) + part

    def query_part(quad):
        g = lax.div(quad, 2)
        part = jnp.dot(kt[g], dst[quad], preferred_element_type=F32)
        dq_ref[:, quad_cols(quad)] = jnp.concatenate(
            [(part[:, i * HD : (i + 1) * HD].T * SCALE).astype(BF) for i in range(4)], axis=1
        )

    def query_out(quad):
        cols = quad_cols(quad)
        return pltpu.make_async_copy(dq_ref.at[:, cols], dq_hbm.at[:, cols], s_out.at[quad])

    def emit_prompt(g):
        dk = dk_acc[keys:total, :] * SCALE
        dv = dv_acc[keys:total, :]
        both = jnp.concatenate(
            (dk.reshape(4 * nz, 8, HD), dv.reshape(4 * nz, 8, HD)), axis=1
        )
        pf[g] = both
        ps[g] = both.astype(BF)
        pc_copy(g).start()

    def emit_resp(g):
        for slot in range(4):
            rows = slice(slot * HD, (slot + 1) * HD)
            dk = dk_acc[rows, :] * SCALE
            dv = dv_acc[rows, :]
            if slot in (0, 2):
                tf[g, slot // 2, 0:HD, :] = dk
                tf[g, slot // 2, HD : 2 * HD, :] = dv
            else:
                tb[g, slot // 2, 0:HD, :] = dk.astype(BF)
                tb[g, slot // 2, HD : 2 * HD, :] = dv.astype(BF)
        tp_copy(g).start()
        tb_copy(g).start()

    half_blocks = 2 * nz

    def pc_copy(g):
        return copy(
            ps.at[g, pl.ds((1 - core) * half_blocks, half_blocks)], rc.at[g], PC, g, peer
        )

    def px_copy(g):
        return copy(xs.at[g], rx.at[g], PX, g, xpeer)

    def px_send(g):
        pc_copy(g).wait_recv()
        away = 1 - x
        xs[g] = (
            pf[g, pl.ds(core * half_blocks + away * nz, nz)]
            + rc[g, pl.ds(away * nz, nz)].astype(F32)
        ).astype(BF)
        xf[g] = (
            pf[g, pl.ds(core * half_blocks + x * nz, nz)] + rc[g, pl.ds(x * nz, nz)].astype(F32)
        )
        px_copy(g).start()

    def near(g, d, slot):
        return copy(zs.at[g, lax.rem(z + d, nz)], rz.at[g, slot], PZ, g, zpeer(d))

    def far(g, d, by, slot):
        return copy(zs.at[g, lax.rem(z + d, nz)], ry.at[g, slot], PY, g, zpeer(by))

    def relay(g, d, slot):
        return copy(ys.at[g, slot], rz.at[g, 6 + slot], PW, g, zpeer(d))

    def pz_send(g):
        px_copy(g).wait_recv()
        sums = xf[g] + rx[g].astype(F32)
        zf[g] = sums
        zs[g] = sums.astype(BF)
        for k in range(1, 5):
            far(g, nz - 4 - k, nz - k, k - 1).start()
        for k in range(1, 4):
            far(g, 4 + k, k, 3 + k).start()
        for k in range(1, 4):
            near(g, k, k - 1).start()
            near(g, nz - k, 2 + k).start()

    def far_all(g):
        return copy(zs.at[g, pl.ds(0, 7)], ry.at[g], PY, g, peer)

    def near_all(g):
        return copy(zs.at[g, pl.ds(0, 6)], rz.at[g, pl.ds(0, 6)], PZ, g, peer)

    def relay_all(g):
        return copy(ys.at[g], rz.at[g, pl.ds(6, 2)], PW, g, peer)

    def pw_send(g):
        far_all(g).wait_recv()
        below = zf[g, lax.rem(z + nz - 4, nz)] + jnp.sum(ry[g, 0:4].astype(F32), axis=0)
        above = zf[g, lax.rem(z + 4, nz)] + jnp.sum(ry[g, 4:7].astype(F32), axis=0)
        ys[g, 0] = below.astype(BF)
        ys[g, 1] = above.astype(BF)
        relay(g, nz - 4, 0).start()
        relay(g, 4, 1).start()

    def prompt_out(g):
        near_all(g).wait_recv()
        relay_all(g).wait_recv()
        sums = zf[g, z] + jnp.sum(rz[g].astype(F32), axis=0)
        cols = slice(g * HD, (g + 1) * HD)
        dpk_ref[:, cols] = sums[0:8]
        dpv_ref[:, cols] = sums[8:16]

    def tp_copy(g):
        return copy(tb.at[g, core], rp.at[g], TP, g, peer)

    def tb_copy(g):
        return copy(tb.at[g, 1 - core], rb.at[g], TB, g, lax.rem(me + n - 3 + 2 * core, n))

    def ta_copy(g):
        return copy(ts.at[g], ra.at[g], TA, g, lax.rem(me + n - 2, n))

    def ts_send(g):
        tp_copy(g).wait_recv()
        ts[g] = (tf[g, 1] + rp[g].astype(F32)).astype(BF)
        ta_copy(g).start()

    def resp_out(g):
        ta_copy(g).wait_recv()
        tb_copy(g).wait_recv()
        sums = tf[g, 0] + ra[g].astype(F32) + rb[g].astype(F32)
        cols = slice(g * HD, (g + 1) * HD)
        drk_ref[:, cols] = sums[0:HD]
        drv_ref[:, cols] = sums[HD : 2 * HD]

    def when(flag, *calls):
        @pl.when(flag)
        def _():
            for call, g in calls:
                call(g)

    def resp_quad(quad):
        resp_half(quad, 0, pr_a, dpr_a)
        resp_half(quad, 1, pr_b, dpr_b)

    kv_ready(0)
    make_bias()

    def resp_step(quad, carry):
        resp_quad(quad)
        when(quad == 0, (ring_step, 3), (kv_forward, 1), (kv_send, 2), (gather_c, 0))
        when(quad == 1, (ring_step, 4))
        return carry

    lax.fori_loop(0, 2, resp_step, 0)
    kv_ready(1)
    prompt_ready(0)
    ring_end()
    for g in range(1, HK):
        gather_x(g)
    resp_quad(2)
    full_quad(0)
    kv_forward(2)
    kv_send(3)
    gather_c(1)

    def both_step(quad, carry):
        when(quad == 4, (kv_ready, 2), (prompt_ready, 1))
        when(quad == 6, (kv_ready, 3), (prompt_ready, 2))
        add_keys(quad - 3, 0, total)
        resp_quad(quad)
        full_quad(quad - 2)
        when(quad == 3, (gather_c, 2))
        when(quad == 4, (emit_prompt, 0), (emit_resp, 0), (kv_forward, 3))
        when(quad == 5, (px_send, 0), (ts_send, 0), (gather_c, 3))
        when(quad == 6, (emit_prompt, 1), (emit_resp, 1), (pz_send, 0))
        when(quad == 7, (px_send, 1), (ts_send, 1), (pw_send, 0))
        return carry

    lax.fori_loop(3, quads, both_step, 0)

    def full_step(quad, carry):
        g = lax.div(quad, 2)
        first = lax.rem(quad, 2) == 0
        when(first, (prompt_ready, g))
        add_keys(quad - 1, 0, total)
        full_quad(quad)
        when(first, (emit_prompt, g - 1), (emit_resp, g - 1), (pz_send, g - 2))
        when(~first, (px_send, g - 1), (ts_send, g - 1), (pw_send, g - 2))
        return carry

    lax.fori_loop(quads - 2, quads, full_step, 0)

    def query(*which):
        for quad in which:
            query_part(quad)
            query_out(quad).start()

    last = HK - 1
    add_keys(quads - 1, keys, total)
    emit_prompt(last)
    add_keys(quads - 1, 0, keys)
    emit_resp(last)
    pz_send(last - 1)
    query(0, 1, 2)
    px_send(last)
    ts_send(last)
    query(3, 4)
    pw_send(last - 1)
    query(5)
    pz_send(last)
    query(6, 7)
    for g in range(last):
        prompt_out(g)
        resp_out(g)
    pw_send(last)
    resp_out(last)
    prompt_out(last)

    sent = gat.at[0, 0, pl.ds(0, nz - 1), pl.ds(1, HK - 1)]
    pltpu.make_async_remote_copy(
        src_ref=sent,
        dst_ref=sent,
        send_sem=s_ring.at[0],
        recv_sem=r_ring.at[0],
        device_id=device(peer),
        device_id_type=MESH,
    ).wait_send()
    for g in range(HK):
        kv_far(g).wait_send()
        kv_side(g).wait_send()
        kv_pass(g).wait_send()
        gx_copy(g).wait_send()
        gc_copy(g).wait_send()
        pc_copy(g).wait_send()
        px_copy(g).wait_send()
        if g == 0:
            gz_all().wait_send()
        near_all(g).wait_send()
        far_all(g).wait_send()
        relay_all(g).wait_send()
        tp_copy(g).wait_send()
        tb_copy(g).wait_send()
        ta_copy(g).wait_send()
    for quad in range(quads):
        query_out(quad).wait()


def hand_over(*refs):
    sems = refs[10]
    copies = [
        pltpu.make_async_copy(refs[i], refs[5 + i], sems.at[i]) for i in range(5)
    ]
    for one in copies:
        one.start()
    for one in copies:
        one.wait()


def on_device(queries, resp_key, resp_value, prompt_key, prompt_value, out_grad, segment):
    n = lax.axis_size("seq")
    nz = n // 4
    rows = queries.shape[0]
    npr = 32 * nz
    total = 4 * HD + npr
    quads = 2 * HK
    vmem = pl.BlockSpec(memory_space=pltpu.VMEM)
    whole = pl.BlockSpec(memory_space=pl.ANY)
    flat = HK * GROUP * HD
    scratch = [
        ((rows, HK * HD), BF),
        ((rows, HK * HD), BF),
        ((8, HK * HD), BF),
        ((8, HK * HD), BF),
        ((1, rows), jnp.int32),
        ((rows, flat), BF),
        ((rows, flat), BF),
        ((rows, flat), BF),
        ((HD, flat), BF),
        ((HD, flat), BF),
        ((HK, 4, 2 * HD + 16, HD), BF),
        ((2, 2, nz, HK, 16, HD), BF),
        ((4, HD, HD), F32),
        ((quads, 4, HD, 2 * HD), F32),
        ((quads, 4, HD, 2 * HD), F32),
        ((quads, 4, HD, 2 * HD), F32),
        ((quads, 4, HD, 2 * HD), F32),
        ((quads, 2, 8, 2 * HD), F32),
        ((quads, 2, 8, 2 * HD), F32),
        ((npr, 2 * HD), F32),
        ((npr, 2 * HD), F32),
        ((npr, 2 * HD), F32),
        ((npr, 2 * HD), F32),
        ((HK, npr, HD), BF),
        ((HK, npr, HD), BF),
        ((HK, HD, total), BF),
        ((total, 4 * HD), BF),
        ((quads, total, 4 * HD), BF),
        ((total, HD), F32),
        ((total, HD), F32),
        ((HK, 4 * nz, 16, HD), BF),
        ((HK, 4 * nz, 16, HD), F32),
        ((HK, 2 * nz, 16, HD), BF),
        ((HK, nz, 16, HD), BF),
        ((HK, nz, 16, HD), F32),
        ((HK, nz, 16, HD), BF),
        ((HK, nz, 16, HD), BF),
        ((HK, nz, 16, HD), F32),
        ((HK, 8, 16, HD), BF),
        ((HK, 7, 16, HD), BF),
        ((HK, 2, 16, HD), BF),
        ((HK, 2, 2 * HD, HD), BF),
        ((HK, 2, 2 * HD, HD), F32),
        ((HK, 2 * HD, HD), BF),
        ((HK, 2 * HD, HD), BF),
        ((HK, 2 * HD, HD), BF),
        ((HK, 2 * HD, HD), BF),
    ]
    shapes = [
        jax.ShapeDtypeStruct((rows, flat), BF),
        jax.ShapeDtypeStruct((rows, HK * HD), F32),
        jax.ShapeDtypeStruct((rows, HK * HD), F32),
        jax.ShapeDtypeStruct((8, HK * HD), F32),
        jax.ShapeDtypeStruct((8, HK * HD), F32),
    ]
    results = pl.pallas_call(
        lambda *refs: body(nz, *refs),
        out_shape=shapes,
        in_specs=[whole] * 7,
        out_specs=[whole] + [vmem] * 4,
        scratch_shapes=[pltpu.VMEM(shape, kind) for shape, kind in scratch]
        + [
            pltpu.SemaphoreType.DMA((HK, 3)),
            pltpu.SemaphoreType.DMA((HK, 4)),
            pltpu.SemaphoreType.DMA((1,)),
            pltpu.SemaphoreType.DMA((nz,)),
            pltpu.SemaphoreType.DMA((11, HK)),
            pltpu.SemaphoreType.DMA((11, HK)),
            pltpu.SemaphoreType.DMA((7,)),
            pltpu.SemaphoreType.DMA((quads,)),
        ],
        compiler_params=pltpu.CompilerParams(
            collective_id=0, has_side_effects=True, vmem_limit_bytes=60 * 1024 * 1024
        ),
        cost_estimate=pl.CostEstimate(
            flops=6 * 10**9, bytes_accessed=6 * 10**6, transcendentals=4 * 10**6
        ),
        name="attention_backward",
    )(
        queries,
        resp_key,
        resp_value,
        prompt_key,
        prompt_value,
        out_grad,
        segment.reshape(1, rows),
    )
    return tuple(
        pl.pallas_call(
            hand_over,
            out_shape=shapes,
            in_specs=[vmem] * 5,
            out_specs=[whole] * 5,
            scratch_shapes=[pltpu.SemaphoreType.DMA((5,))],
            cost_estimate=pl.CostEstimate(
                flops=0, bytes_accessed=3 * 10**6, transcendentals=0
            ),
            name="hand_over",
        )(*results)
    )


def solution(mesh):
    spec = P(("grp", "seq"), None)
    return jax.shard_map(
        on_device,
        mesh=mesh,
        in_specs=(spec,) * 6 + (P(("grp", "seq")),),
        out_specs=(spec,) * 5,
        check_vma=False,
    )
```

```python
import jax
import jax.numpy as jnp
from jax import lax
from jax.experimental import pallas as pl
from jax.experimental.pallas import tpu as pltpu
from jax.sharding import PartitionSpec as P

MESH = pl.DeviceIdType.MESH
HD = 128
HK = 4
GROUP = 8
PAIRS = GROUP // 2
SCALE = HD ** (-0.5)
BF = jnp.bfloat16
F32 = jnp.float32


def body(
    nz,
    q_hbm,
    rk_hbm,
    rv_hbm,
    pk_hbm,
    pv_hbm,
    do_hbm,
    seg_hbm,
    dq_hbm,
    drk_ref,
    drv_ref,
    dpk_ref,
    dpv_ref,
    rk_ref,
    rv_ref,
    pk_ref,
    pv_ref,
    seg_ref,
    q_ref,
    do_ref,
    dq_ref,
    qt,
    dot,
    win,
    gat,
    bias,
    pr_a,
    pr_b,
    dpr_a,
    dpr_b,
    mr,
    lr,
    sp_a,
    sp_b,
    dpp_a,
    dpp_b,
    kp,
    vp,
    kt,
    pt,
    dst,
    dk_acc,
    dv_acc,
    ps,
    pf,
    rc,
    xs,
    xf,
    rx,
    zs,
    zf,
    rz,
    ry,
    ys,
    tb,
    tf,
    rp,
    ts,
    ra,
    rb,
    s_kv,
    r_kv,
    s_ring,
    r_ring,
    s_one,
    r_one,
    s_in,
    s_out,
):
    n = 4 * nz
    keys = 4 * HD
    npr = 32 * nz
    total = keys + npr
    quads = 2 * HK
    wide = 4 * HD
    me = lax.axis_index("seq")
    grp = lax.axis_index("grp")
    core = lax.rem(me, 2)
    x = lax.rem(lax.div(me, 2), 2)
    z = lax.div(me, 4)
    peer = me + 1 - 2 * core
    xpeer = me + 2 - 4 * x

    def zpeer(d):
        return lax.rem(me + 4 * d, n)

    def device(index):
        return (grp, index)

    GX, GC, PC, PX, PZ, PY, PW, TP, TB, TA = range(10)

    def copy(src, dst, kind, g, to):
        return pltpu.make_async_remote_copy(
            src_ref=src,
            dst_ref=dst,
            send_sem=s_one.at[kind, g],
            recv_sem=r_one.at[kind, g],
            device_id=device(to),
            device_id_type=MESH,
        )

    small = [
        pltpu.make_async_copy(source, target, s_in.at[2 + i])
        for i, (source, target) in enumerate(
            (
                (rk_hbm, rk_ref),
                (rv_hbm, rv_ref),
                (pk_hbm, pk_ref),
                (pv_hbm, pv_ref),
                (seg_hbm, seg_ref),
            )
        )
    ]
    q_in = pltpu.make_async_copy(q_hbm, q_ref, s_in.at[0])
    do_in = pltpu.make_async_copy(do_hbm, do_ref, s_in.at[1])
    for one in (*small, q_in, do_in):
        one.start()

    barrier = pltpu.get_barrier_semaphore()

    def greet(to):
        pl.semaphore_signal(barrier, inc=1, device_id=device(to), device_id_type=MESH)

    greet(peer)
    greet(xpeer)
    greet(lax.rem(me + 2, n))
    greet(lax.rem(me + n - 2, n))
    greet(lax.rem(me + n + 6 * core - 3, n))

    for d in range(1, 5):
        greet(zpeer(d))
        greet(zpeer(nz - d))
    for one in small:
        one.wait()

    labels = jnp.broadcast_to((seg_ref[...] + 1).astype(F32), (16, HD)).astype(BF)
    for g in range(HK):
        cols = slice(g * HD, (g + 1) * HD)
        win[g, 0, 0:HD, :] = rk_ref[:, cols]
        win[g, 0, HD : 2 * HD, :] = rv_ref[:, cols]
        win[g, 0, 2 * HD : 2 * HD + 16, :] = labels
        gat[core, x, z, g] = jnp.concatenate(
            (pk_ref[:, cols].astype(F32), pv_ref[:, cols].astype(F32)), axis=0
        ).astype(BF)
    pl.semaphore_wait(barrier, 13)

    def kv_copy(g, which, from_slot, to_slot, to):
        part = pl.ds(0, 2 * HD + (16 if g == 0 else 0))
        return pltpu.make_async_remote_copy(
            src_ref=win.at[g, from_slot, part],
            dst_ref=win.at[g, to_slot, part],
            send_sem=s_kv.at[g, which],
            recv_sem=r_kv.at[g, to_slot],
            device_id=device(to),
            device_id_type=MESH,
        )

    def kv_far(g):
        return kv_copy(g, 0, 0, 2, lax.rem(me + 2, n))

    def kv_side(g):
        return kv_copy(g, 1, 0, 1 + 2 * core, lax.rem(me + 1 + 2 * core, n))

    def kv_pass(g):
        return kv_copy(g, 2, 2, 3 - 2 * core, peer)

    def kv_forward(g):
        kv_far(g).wait_recv()
        kv_pass(g).start()

    def kv_ready(g):
        kv_copy(g, 1, 0, 1, peer).wait_recv()
        kv_copy(g, 1, 0, 3, peer).wait_recv()

    steps = nz // 4

    def ring_copy(owner, to, d):
        part = gat.at[core, x, owner]
        return pltpu.make_async_remote_copy(
            src_ref=part,
            dst_ref=part,
            send_sem=s_ring.at[0],
            recv_sem=r_ring.at[d],
            device_id=device(to),
            device_id_type=MESH,
        )

    def ring_wait(d):
        ring_copy(lax.rem(z + nz - d, nz), peer, d).wait_recv()

    def ring_step(k):
        if k > 1:
            ring_wait(2 * (k - 1))
            ring_wait(nz - 2 * (k - 1))
        up = lax.rem(z + nz - 2 * (k - 1), nz)
        down = lax.rem(z + 2 * (k - 1), nz)
        ring_copy(up, zpeer(2), 2 * k).start()
        if k < steps:
            ring_copy(down, zpeer(nz - 2), nz - 2 * k).start()
        ring_copy(up, zpeer(1), 2 * k - 1).start()
        ring_copy(down, zpeer(nz - 1), nz - 2 * k + 1).start()

    def gx_copy(g):
        part = gat.at[core, x, pl.ds(0, nz), g]
        return copy(part, part, GX, g, xpeer)

    def gc_copy(g):
        part = gat.at[core, pl.ds(0, 2), pl.ds(0, nz), g]
        return copy(part, part, GC, g, peer)

    def ring_end():
        for k in range(1, steps + 1):
            ring_wait(2 * k - 1)
            ring_wait(nz - 2 * k + 1)
        ring_wait(2 * steps)

    def gather_x(g):
        gx_copy(g).start()

    def gather_c(g):
        gx_copy(g).wait_recv()
        gc_copy(g).start()

    def kv_send(g):
        kv_far(g).start()
        kv_side(g).start()

    kv_send(0)
    ring_step(1)

    q_in.wait()
    do_in.wait()

    def flip(h, carry):
        for i in range(4):
            cols = pl.ds(pl.multiple_of((h * 4 + i) * HD, HD), HD)
            qt[:, cols] = q_ref[:, cols].T
            dot[:, cols] = do_ref[:, cols].T
        return carry

    lax.fori_loop(0, HK * GROUP // 8, flip, 0)
    kv_send(1)
    ring_step(2)
    lax.fori_loop(HK * GROUP // 8, HK * GROUP // 4, flip, 0)
    kv_forward(0)
    kv_send(2)
    ring_step(3)

    def make_bias():
        mine = jnp.broadcast_to(win[0, 0, 2 * HD : 2 * HD + 16, :].astype(F32)[0:1], (HD, HD))
        row = lax.broadcasted_iota(jnp.int32, (HD, HD), 1)
        col = lax.broadcasted_iota(jnp.int32, (HD, HD), 0)
        for slot in range(4):
            theirs = jnp.broadcast_to(
                win[0, slot, 2 * HD : 2 * HD + 16, :].astype(F32)[0:1], (HD, HD)
            ).T
            seen = mine == theirs
            if slot == 0:
                seen = seen & (col <= row)
            else:
                seen = seen & (jnp.broadcast_to(me, (HD, HD)) >= slot)
            bias[slot] = jnp.where(seen, 0.0, -jnp.inf)

    def fold(value, op):
        return op(value.reshape(value.shape[0] // 8, 8, value.shape[1]), axis=0)

    def half_cols(quad, half):
        return pl.ds(pl.multiple_of(quad * wide + half * 2 * HD, 2 * HD), 2 * HD)

    def quad_cols(quad):
        return pl.ds(pl.multiple_of(quad * wide, wide), wide)

    def resp_half(quad, half, pr, dpr):
        g = lax.div(quad, 2)
        cols = half_cols(quad, half)
        k4 = win[g, :, 0:HD, :].reshape(keys, HD)
        v4 = win[g, :, HD : 2 * HD, :].reshape(keys, HD)
        scores = jnp.dot(k4, qt[:, cols], preferred_element_type=F32)
        high = None
        for slot in range(4):
            mask = bias[slot]
            part = scores[slot * HD : (slot + 1) * HD] + jnp.concatenate((mask, mask), axis=1)
            pr[quad, slot] = part
            top = fold(part, jnp.max)
            high = top if high is None else jnp.maximum(high, top)
        high = jnp.max(high, axis=0, keepdims=True)
        dpr[quad] = jnp.dot(v4, dot[:, cols], preferred_element_type=F32).reshape(4, HD, 2 * HD)
        low = None
        for slot in range(4):
            part = jnp.exp((pr[quad, slot] - high) * SCALE)
            pr[quad, slot] = part
            add = fold(part, jnp.sum)
            low = add if low is None else low + add
        mr[quad, half] = jnp.broadcast_to(high, (8, 2 * HD))
        lr[quad, half] = jnp.broadcast_to(jnp.sum(low, axis=0, keepdims=True), (8, 2 * HD))

    def prompt_ready(g):
        gc_copy(g).wait_recv()
        all_rows = gat[:, :, :, g].reshape(4 * nz, 16, HD).astype(F32)
        kp[g] = all_rows[:, 0:8].reshape(npr, HD).astype(BF)
        vp[g] = all_rows[:, 8:16].reshape(npr, HD).astype(BF)
        for slot in range(4):
            kt[g, :, slot * HD : (slot + 1) * HD] = win[g, slot, 0:HD, :].T
        for lower in range(0, npr, HD):
            kt[g, :, keys + lower : keys + lower + HD] = kp[g, lower : lower + HD, :].T

    chunks = npr // HD

    def full_half(quad, half, pr, dpr, sp, dpp):
        g = lax.div(quad, 2)
        cols = half_cols(quad, half)
        own = slice(half * 2 * HD, (half + 1) * 2 * HD)
        scores = jnp.dot(kp[g], qt[:, cols], preferred_element_type=F32)
        sp[...] = scores
        high = jnp.maximum(mr[quad, half], fold(scores, jnp.max))
        dpp[...] = jnp.dot(vp[g], dot[:, cols], preferred_element_type=F32)
        old = mr[quad, half][0:1]
        high = jnp.max(high, axis=0, keepdims=True)
        low = None
        for c in range(chunks):
            rows = slice(c * HD, (c + 1) * HD)
            part = jnp.exp((sp[rows, :] - high) * SCALE)
            sp[rows, :] = part
            add = fold(part, jnp.sum)
            low = add if low is None else low + add
        shrink = jnp.exp((old - high) * SCALE)
        sums = jnp.sum(low, axis=0, keepdims=True) + lr[quad, half][0:1] * shrink
        f_prompt = 1.0 / sums
        f_resp = shrink * f_prompt
        delta = None
        for slot in range(4):
            rounded = (pr[quad, slot] * f_resp).astype(BF)
            pt[slot * HD : (slot + 1) * HD, own] = rounded
            add = fold(rounded.astype(F32) * dpr[quad, slot], jnp.sum)
            delta = add if delta is None else delta + add
        for c in range(chunks):
            rows = slice(c * HD, (c + 1) * HD)
            rounded = (sp[rows, :] * f_prompt).astype(BF)
            pt[keys + c * HD : keys + (c + 1) * HD, own] = rounded
            delta = delta + fold(rounded.astype(F32) * dpp[rows, :], jnp.sum)
        delta = jnp.sum(delta, axis=0, keepdims=True)
        for slot in range(4):
            dst[quad, slot * HD : (slot + 1) * HD, own] = (
                (pr[quad, slot] * f_resp) * (dpr[quad, slot] - delta)
            ).astype(BF)
        for c in range(chunks):
            rows = slice(c * HD, (c + 1) * HD)
            dst[quad, keys + c * HD : keys + (c + 1) * HD, own] = (
                (sp[rows, :] * f_prompt) * (dpp[rows, :] - delta)
            ).astype(BF)

    def full_quad(quad):
        full_half(quad, 0, pr_a, dpr_a, sp_a, dpp_a)
        full_half(quad, 1, pr_b, dpr_b, sp_b, dpp_b)

    def rows_of(ref, quad):
        part = ref[:, quad_cols(quad)]
        return jnp.concatenate([part[:, i * HD : (i + 1) * HD] for i in range(4)], axis=0)

    def add_keys(quad, lower, upper):
        second = lax.rem(quad, 2) == 1
        rows = slice(lower, upper)
        for acc, left, right in ((dv_acc, pt, do_ref), (dk_acc, dst.at[quad], q_ref)):
            part = jnp.dot(left[rows, :], rows_of(right, quad), preferred_element_type=F32)
            acc[rows, :] = jnp.where(second, acc[rows, :], 0.0) + part

    def query_part(quad):
        g = lax.div(quad, 2)
        part = jnp.dot(kt[g], dst[quad], preferred_element_type=F32)
        dq_ref[:, quad_cols(quad)] = jnp.concatenate(
            [(part[:, i * HD : (i + 1) * HD].T * SCALE).astype(BF) for i in range(4)], axis=1
        )

    def query_out(quad):
        cols = quad_cols(quad)
        return pltpu.make_async_copy(dq_ref.at[:, cols], dq_hbm.at[:, cols], s_out.at[quad])

    def emit_prompt(g):
        dk = dk_acc[keys:total, :] * SCALE
        dv = dv_acc[keys:total, :]
        both = jnp.concatenate(
            (dk.reshape(4 * nz, 8, HD), dv.reshape(4 * nz, 8, HD)), axis=1
        )
        pf[g] = both
        ps[g] = both.astype(BF)
        pc_copy(g).start()

    def emit_resp(g):
        for slot in range(4):
            rows = slice(slot * HD, (slot + 1) * HD)
            dk = dk_acc[rows, :] * SCALE
            dv = dv_acc[rows, :]
            if slot in (0, 2):
                tf[g, slot // 2, 0:HD, :] = dk
                tf[g, slot // 2, HD : 2 * HD, :] = dv
            else:
                tb[g, slot // 2, 0:HD, :] = dk.astype(BF)
                tb[g, slot // 2, HD : 2 * HD, :] = dv.astype(BF)
        tp_copy(g).start()
        tb_copy(g).start()

    half_blocks = 2 * nz

    def pc_copy(g):
        return copy(
            ps.at[g, pl.ds((1 - core) * half_blocks, half_blocks)], rc.at[g], PC, g, peer
        )

    def px_copy(g):
        return copy(xs.at[g], rx.at[g], PX, g, xpeer)

    def px_send(g):
        pc_copy(g).wait_recv()
        away = 1 - x
        xs[g] = (
            pf[g, pl.ds(core * half_blocks + away * nz, nz)]
            + rc[g, pl.ds(away * nz, nz)].astype(F32)
        ).astype(BF)
        xf[g] = (
            pf[g, pl.ds(core * half_blocks + x * nz, nz)] + rc[g, pl.ds(x * nz, nz)].astype(F32)
        )
        px_copy(g).start()

    def near(g, d, slot):
        return copy(zs.at[g, lax.rem(z + d, nz)], rz.at[g, slot], PZ, g, zpeer(d))

    def far(g, d, by, slot):
        return copy(zs.at[g, lax.rem(z + d, nz)], ry.at[g, slot], PY, g, zpeer(by))

    def relay(g, d, slot):
        return copy(ys.at[g, slot], rz.at[g, 6 + slot], PW, g, zpeer(d))

    def pz_send(g):
        px_copy(g).wait_recv()
        sums = xf[g] + rx[g].astype(F32)
        zf[g] = sums
        zs[g] = sums.astype(BF)
        for k in range(1, 5):
            far(g, nz - 4 - k, nz - k, k - 1).start()
        for k in range(1, 4):
            far(g, 4 + k, k, 3 + k).start()
        for k in range(1, 4):
            near(g, k, k - 1).start()
            near(g, nz - k, 2 + k).start()

    def far_all(g):
        return copy(zs.at[g, pl.ds(0, 7)], ry.at[g], PY, g, peer)

    def near_all(g):
        return copy(zs.at[g, pl.ds(0, 6)], rz.at[g, pl.ds(0, 6)], PZ, g, peer)

    def relay_all(g):
        return copy(ys.at[g], rz.at[g, pl.ds(6, 2)], PW, g, peer)

    def pw_send(g):
        far_all(g).wait_recv()
        below = zf[g, lax.rem(z + nz - 4, nz)] + jnp.sum(ry[g, 0:4].astype(F32), axis=0)
        above = zf[g, lax.rem(z + 4, nz)] + jnp.sum(ry[g, 4:7].astype(F32), axis=0)
        ys[g, 0] = below.astype(BF)
        ys[g, 1] = above.astype(BF)
        relay(g, nz - 4, 0).start()
        relay(g, 4, 1).start()

    def prompt_out(g):
        near_all(g).wait_recv()
        relay_all(g).wait_recv()
        sums = zf[g, z] + jnp.sum(rz[g].astype(F32), axis=0)
        cols = slice(g * HD, (g + 1) * HD)
        dpk_ref[:, cols] = sums[0:8]
        dpv_ref[:, cols] = sums[8:16]

    def tp_copy(g):
        return copy(tb.at[g, core], rp.at[g], TP, g, peer)

    def tb_copy(g):
        return copy(tb.at[g, 1 - core], rb.at[g], TB, g, lax.rem(me + n - 3 + 2 * core, n))

    def ta_copy(g):
        return copy(ts.at[g], ra.at[g], TA, g, lax.rem(me + n - 2, n))

    def ts_send(g):
        tp_copy(g).wait_recv()
        ts[g] = (tf[g, 1] + rp[g].astype(F32)).astype(BF)
        ta_copy(g).start()

    def resp_out(g):
        ta_copy(g).wait_recv()
        tb_copy(g).wait_recv()
        sums = tf[g, 0] + ra[g].astype(F32) + rb[g].astype(F32)
        cols = slice(g * HD, (g + 1) * HD)
        drk_ref[:, cols] = sums[0:HD]
        drv_ref[:, cols] = sums[HD : 2 * HD]

    def when(flag, *calls):
        @pl.when(flag)
        def _():
            for call, g in calls:
                call(g)

    def resp_quad(quad):
        resp_half(quad, 0, pr_a, dpr_a)
        resp_half(quad, 1, pr_b, dpr_b)

    kv_ready(0)
    make_bias()

    def resp_step(quad, carry):
        when(quad == 2, (kv_ready, 1))
        resp_quad(quad)
        when(quad == 0, (ring_step, 4), (kv_forward, 1), (kv_send, 3))

        @pl.when(quad == 1)
        def _():
            ring_end()
            for g in range(HK):
                gather_x(g)

        when(quad == 2, (kv_forward, 2))
        when(quad == 3, (gather_c, 0))
        return carry

    lax.fori_loop(0, 4, resp_step, 0)
    kv_ready(2)
    prompt_ready(0)
    resp_quad(4)
    full_quad(0)
    gather_c(1)

    def both_step(quad, carry):
        when(quad == 6, (kv_ready, 3), (prompt_ready, 1))
        add_keys(quad - 5, 0, total)
        resp_quad(quad)
        full_quad(quad - 4)
        when(quad == 5, (kv_forward, 3))
        when(quad == 6, (emit_prompt, 0), (emit_resp, 0), (gather_c, 2))
        when(quad == 7, (gather_c, 3), (px_send, 0), (ts_send, 0))
        return carry

    lax.fori_loop(5, quads, both_step, 0)

    def full_step(quad, carry):
        g = lax.div(quad, 2)
        first = lax.rem(quad, 2) == 0
        when(first, (prompt_ready, g))
        add_keys(quad - 1, 0, total)
        full_quad(quad)
        when(first, (emit_prompt, g - 1), (emit_resp, g - 1), (pz_send, g - 2))
        when(~first, (px_send, g - 1), (ts_send, g - 1), (pw_send, g - 2))
        return carry

    lax.fori_loop(4, quads, full_step, 0)

    def query(*which):
        for quad in which:
            query_part(quad)
            query_out(quad).start()

    last = HK - 1
    add_keys(quads - 1, keys, total)
    emit_prompt(last)
    add_keys(quads - 1, 0, keys)
    emit_resp(last)
    pz_send(last - 1)
    query(0, 1, 2)
    px_send(last)
    ts_send(last)
    query(3, 4)
    pw_send(last - 1)
    query(5)
    pz_send(last)
    query(6, 7)
    for g in range(last):
        prompt_out(g)
        resp_out(g)
    pw_send(last)
    resp_out(last)
    prompt_out(last)

    sent = gat.at[0, 0, pl.ds(0, nz - 1)]
    pltpu.make_async_remote_copy(
        src_ref=sent,
        dst_ref=sent,
        send_sem=s_ring.at[0],
        recv_sem=r_ring.at[0],
        device_id=device(peer),
        device_id_type=MESH,
    ).wait_send()
    for g in range(HK):
        kv_far(g).wait_send()
        kv_side(g).wait_send()
        kv_pass(g).wait_send()
        gx_copy(g).wait_send()
        gc_copy(g).wait_send()
        pc_copy(g).wait_send()
        px_copy(g).wait_send()
        near_all(g).wait_send()
        far_all(g).wait_send()
        relay_all(g).wait_send()
        tp_copy(g).wait_send()
        tb_copy(g).wait_send()
        ta_copy(g).wait_send()
    for quad in range(quads):
        query_out(quad).wait()


PIECES = ((0, 4), (1, 1), (2, 1), (3, 1), (4, 1))


def hand_over(*refs):
    sources, targets, held, sems = refs[:5], refs[5:10], refs[10:15], refs[15]
    loads, stores = [], []
    for index, count in PIECES:
        rows = sources[index].shape[0] // count
        for i in range(count):
            part = pl.ds(i * rows, rows)
            here = held[index].at[part]
            slot = len(loads)
            loads.append(
                pltpu.make_async_copy(sources[index].at[part], here, sems.at[0, slot])
            )
            stores.append(
                pltpu.make_async_copy(here, targets[index].at[part], sems.at[1, slot])
            )
    for load in loads:
        load.start()
    for load, store in zip(loads, stores):
        load.wait()
        store.start()
    for store in stores:
        store.wait()


def on_device(queries, resp_key, resp_value, prompt_key, prompt_value, out_grad, segment):
    n = lax.axis_size("seq")
    nz = n // 4
    rows = queries.shape[0]
    npr = 32 * nz
    total = 4 * HD + npr
    quads = 2 * HK
    vmem = pl.BlockSpec(memory_space=pltpu.VMEM)
    whole = pl.BlockSpec(memory_space=pl.ANY)
    flat = HK * GROUP * HD
    scratch = [
        ((rows, HK * HD), BF),
        ((rows, HK * HD), BF),
        ((8, HK * HD), BF),
        ((8, HK * HD), BF),
        ((1, rows), jnp.int32),
        ((rows, flat), BF),
        ((rows, flat), BF),
        ((rows, flat), BF),
        ((HD, flat), BF),
        ((HD, flat), BF),
        ((HK, 4, 2 * HD + 16, HD), BF),
        ((2, 2, nz, HK, 16, HD), BF),
        ((4, HD, HD), F32),
        ((quads, 4, HD, 2 * HD), F32),
        ((quads, 4, HD, 2 * HD), F32),
        ((quads, 4, HD, 2 * HD), F32),
        ((quads, 4, HD, 2 * HD), F32),
        ((quads, 2, 8, 2 * HD), F32),
        ((quads, 2, 8, 2 * HD), F32),
        ((npr, 2 * HD), F32),
        ((npr, 2 * HD), F32),
        ((npr, 2 * HD), F32),
        ((npr, 2 * HD), F32),
        ((HK, npr, HD), BF),
        ((HK, npr, HD), BF),
        ((HK, HD, total), BF),
        ((total, 4 * HD), BF),
        ((quads, total, 4 * HD), BF),
        ((total, HD), F32),
        ((total, HD), F32),
        ((HK, 4 * nz, 16, HD), BF),
        ((HK, 4 * nz, 16, HD), F32),
        ((HK, 2 * nz, 16, HD), BF),
        ((HK, nz, 16, HD), BF),
        ((HK, nz, 16, HD), F32),
        ((HK, nz, 16, HD), BF),
        ((HK, nz, 16, HD), BF),
        ((HK, nz, 16, HD), F32),
        ((HK, 8, 16, HD), BF),
        ((HK, 7, 16, HD), BF),
        ((HK, 2, 16, HD), BF),
        ((HK, 2, 2 * HD, HD), BF),
        ((HK, 2, 2 * HD, HD), F32),
        ((HK, 2 * HD, HD), BF),
        ((HK, 2 * HD, HD), BF),
        ((HK, 2 * HD, HD), BF),
        ((HK, 2 * HD, HD), BF),
    ]
    shapes = [
        jax.ShapeDtypeStruct((rows, flat), BF),
        jax.ShapeDtypeStruct((rows, HK * HD), F32),
        jax.ShapeDtypeStruct((rows, HK * HD), F32),
        jax.ShapeDtypeStruct((8, HK * HD), F32),
        jax.ShapeDtypeStruct((8, HK * HD), F32),
    ]
    results = pl.pallas_call(
        lambda *refs: body(nz, *refs),
        out_shape=shapes,
        in_specs=[whole] * 7,
        out_specs=[whole] + [vmem] * 4,
        scratch_shapes=[pltpu.VMEM(shape, kind) for shape, kind in scratch]
        + [
            pltpu.SemaphoreType.DMA((HK, 3)),
            pltpu.SemaphoreType.DMA((HK, 4)),
            pltpu.SemaphoreType.DMA((1,)),
            pltpu.SemaphoreType.DMA((nz,)),
            pltpu.SemaphoreType.DMA((10, HK)),
            pltpu.SemaphoreType.DMA((10, HK)),
            pltpu.SemaphoreType.DMA((7,)),
            pltpu.SemaphoreType.DMA((quads,)),
        ],
        compiler_params=pltpu.CompilerParams(
            collective_id=0, has_side_effects=True, vmem_limit_bytes=60 * 1024 * 1024
        ),
        cost_estimate=pl.CostEstimate(
            flops=6 * 10**9, bytes_accessed=6 * 10**6, transcendentals=4 * 10**6
        ),
        name="attention_backward",
    )(
        queries,
        resp_key,
        resp_value,
        prompt_key,
        prompt_value,
        out_grad,
        segment.reshape(1, rows),
    )
    return tuple(
        pl.pallas_call(
            hand_over,
            out_shape=shapes,
            in_specs=[whole] * 5,
            out_specs=[whole] * 5,
            scratch_shapes=[pltpu.VMEM(one.shape, one.dtype) for one in shapes]
            + [pltpu.SemaphoreType.DMA((2, sum(count for _, count in PIECES)))],
            compiler_params=pltpu.CompilerParams(vmem_limit_bytes=60 * 1024 * 1024),
            cost_estimate=pl.CostEstimate(
                flops=0, bytes_accessed=3 * 10**6, transcendentals=0
            ),
            name="hand_over",
        )(*results)
    )


def solution(mesh):
    spec = P(("grp", "seq"), None)
    return jax.shard_map(
        on_device,
        mesh=mesh,
        in_specs=(spec,) * 6 + (P(("grp", "seq")),),
        out_specs=(spec,) * 5,
        check_vma=False,
    )
```

```python
import jax
import jax.numpy as jnp
from jax import lax
from jax.experimental import pallas as pl
from jax.experimental.pallas import tpu as pltpu
from jax.sharding import PartitionSpec as P

MESH = pl.DeviceIdType.MESH
HD = 128
HK = 4
GROUP = 8
PAIRS = GROUP // 2
SCALE = HD ** (-0.5)
BF = jnp.bfloat16
F32 = jnp.float32


def body(
    nz,
    q_hbm,
    rk_hbm,
    rv_hbm,
    pk_hbm,
    pv_hbm,
    do_hbm,
    seg_hbm,
    dq_hbm,
    drk_ref,
    drv_ref,
    dpk_ref,
    dpv_ref,
    rk_ref,
    rv_ref,
    pk_ref,
    pv_ref,
    seg_ref,
    q_ref,
    do_ref,
    dq_ref,
    qt,
    dot,
    win,
    gat,
    bias,
    pr_a,
    pr_b,
    dpr_a,
    dpr_b,
    mr,
    lr,
    sp_a,
    sp_b,
    dpp_a,
    dpp_b,
    kp,
    vp,
    kt,
    pt,
    dst,
    dk_acc,
    dv_acc,
    ps,
    pf,
    rc,
    xs,
    xf,
    rx,
    zs,
    zf,
    rz,
    ry,
    ys,
    tb,
    tf,
    rp,
    ts,
    ra,
    rb,
    s_kv,
    r_kv,
    s_ring,
    r_ring,
    s_one,
    r_one,
    s_in,
    s_out,
):
    n = 4 * nz
    keys = 4 * HD
    npr = 32 * nz
    total = keys + npr
    quads = 2 * HK
    wide = 4 * HD
    me = lax.axis_index("seq")
    grp = lax.axis_index("grp")
    core = lax.rem(me, 2)
    x = lax.rem(lax.div(me, 2), 2)
    z = lax.div(me, 4)
    peer = me + 1 - 2 * core
    xpeer = me + 2 - 4 * x

    def zpeer(d):
        return lax.rem(me + 4 * d, n)

    def device(index):
        return (grp, index)

    GX, GC, PC, PX, PZ, PY, PW, TP, TB, TA = range(10)

    def copy(src, dst, kind, g, to):
        return pltpu.make_async_remote_copy(
            src_ref=src,
            dst_ref=dst,
            send_sem=s_one.at[kind, g],
            recv_sem=r_one.at[kind, g],
            device_id=device(to),
            device_id_type=MESH,
        )

    small = [
        pltpu.make_async_copy(source, target, s_in.at[2 + i])
        for i, (source, target) in enumerate(
            (
                (rk_hbm, rk_ref),
                (rv_hbm, rv_ref),
                (pk_hbm, pk_ref),
                (pv_hbm, pv_ref),
                (seg_hbm, seg_ref),
            )
        )
    ]
    q_in = pltpu.make_async_copy(q_hbm, q_ref, s_in.at[0])
    do_in = pltpu.make_async_copy(do_hbm, do_ref, s_in.at[1])
    for one in (*small, q_in, do_in):
        one.start()

    barrier = pltpu.get_barrier_semaphore()

    def greet(to):
        pl.semaphore_signal(barrier, inc=1, device_id=device(to), device_id_type=MESH)

    greet(peer)
    greet(xpeer)
    greet(lax.rem(me + 2, n))
    greet(lax.rem(me + n - 2, n))
    greet(lax.rem(me + n + 6 * core - 3, n))

    for d in range(1, 5):
        greet(zpeer(d))
        greet(zpeer(nz - d))
    for one in small:
        one.wait()

    labels = jnp.broadcast_to((seg_ref[...] + 1).astype(F32), (16, HD)).astype(BF)
    for g in range(HK):
        cols = slice(g * HD, (g + 1) * HD)
        win[g, 0, 0:HD, :] = rk_ref[:, cols]
        win[g, 0, HD : 2 * HD, :] = rv_ref[:, cols]
        win[g, 0, 2 * HD : 2 * HD + 16, :] = labels
        gat[core, x, g, z] = jnp.concatenate(
            (pk_ref[:, cols].astype(F32), pv_ref[:, cols].astype(F32)), axis=0
        ).astype(BF)
    pl.semaphore_wait(barrier, 13)

    def kv_copy(g, which, from_slot, to_slot, to):
        part = pl.ds(0, 2 * HD + (16 if g == 0 else 0))
        return pltpu.make_async_remote_copy(
            src_ref=win.at[g, from_slot, part],
            dst_ref=win.at[g, to_slot, part],
            send_sem=s_kv.at[g, which],
            recv_sem=r_kv.at[g, to_slot],
            device_id=device(to),
            device_id_type=MESH,
        )

    def kv_far(g):
        return kv_copy(g, 0, 0, 2, lax.rem(me + 2, n))

    def kv_side(g):
        return kv_copy(g, 1, 0, 1 + 2 * core, lax.rem(me + 1 + 2 * core, n))

    def kv_pass(g):
        return kv_copy(g, 2, 2, 3 - 2 * core, peer)

    def kv_forward(g):
        kv_far(g).wait_recv()
        kv_pass(g).start()

    def kv_ready(g):
        kv_copy(g, 1, 0, 1, peer).wait_recv()
        kv_copy(g, 1, 0, 3, peer).wait_recv()

    steps = nz // 4

    def ring_copy(owner, to, d):
        part = gat.at[core, x, pl.ds(0, HK), owner]
        return pltpu.make_async_remote_copy(
            src_ref=part,
            dst_ref=part,
            send_sem=s_ring.at[0],
            recv_sem=r_ring.at[d],
            device_id=device(to),
            device_id_type=MESH,
        )

    def ring_wait(d):
        ring_copy(lax.rem(z + nz - d, nz), peer, d).wait_recv()

    def ring_step(k):
        if k > 1:
            ring_wait(2 * (k - 1))
            ring_wait(nz - 2 * (k - 1))
        up = lax.rem(z + nz - 2 * (k - 1), nz)
        down = lax.rem(z + 2 * (k - 1), nz)
        ring_copy(up, zpeer(2), 2 * k).start()
        if k < steps:
            ring_copy(down, zpeer(nz - 2), nz - 2 * k).start()
        ring_copy(up, zpeer(1), 2 * k - 1).start()
        ring_copy(down, zpeer(nz - 1), nz - 2 * k + 1).start()

    def gx_copy(g):
        part = gat.at[core, x, g]
        return copy(part, part, GX, g, xpeer)

    def gc_copy(g):
        part = gat.at[core, pl.ds(0, 2), g]
        return copy(part, part, GC, g, peer)

    def ring_end():
        for k in range(1, steps + 1):
            ring_wait(2 * k - 1)
            ring_wait(nz - 2 * k + 1)
        ring_wait(2 * steps)

    def gather_x(g):
        gx_copy(g).start()

    def gather_c(g):
        gx_copy(g).wait_recv()
        gc_copy(g).start()

    def kv_send(g):
        kv_far(g).start()
        kv_side(g).start()

    kv_send(0)
    ring_step(1)

    q_in.wait()
    do_in.wait()

    def flip(h, carry):
        for i in range(4):
            cols = pl.ds(pl.multiple_of((h * 4 + i) * HD, HD), HD)
            qt[:, cols] = q_ref[:, cols].T
            dot[:, cols] = do_ref[:, cols].T
        return carry

    lax.fori_loop(0, HK * GROUP // 8, flip, 0)
    kv_send(1)
    ring_step(2)
    lax.fori_loop(HK * GROUP // 8, HK * GROUP // 4, flip, 0)
    kv_forward(0)
    kv_send(2)
    ring_step(3)

    def make_bias():
        mine = jnp.broadcast_to(win[0, 0, 2 * HD : 2 * HD + 16, :].astype(F32)[0:1], (HD, HD))
        row = lax.broadcasted_iota(jnp.int32, (HD, HD), 1)
        col = lax.broadcasted_iota(jnp.int32, (HD, HD), 0)
        for slot in range(4):
            theirs = jnp.broadcast_to(
                win[0, slot, 2 * HD : 2 * HD + 16, :].astype(F32)[0:1], (HD, HD)
            ).T
            seen = mine == theirs
            if slot == 0:
                seen = seen & (col <= row)
            else:
                seen = seen & (jnp.broadcast_to(me, (HD, HD)) >= slot)
            bias[slot] = jnp.where(seen, 0.0, -jnp.inf)

    def fold(value, op):
        return op(value.reshape(value.shape[0] // 8, 8, value.shape[1]), axis=0)

    def half_cols(quad, half):
        return pl.ds(pl.multiple_of(quad * wide + half * 2 * HD, 2 * HD), 2 * HD)

    def quad_cols(quad):
        return pl.ds(pl.multiple_of(quad * wide, wide), wide)

    def resp_half(quad, half, pr, dpr):
        g = lax.div(quad, 2)
        cols = half_cols(quad, half)
        k4 = win[g, :, 0:HD, :].reshape(keys, HD)
        v4 = win[g, :, HD : 2 * HD, :].reshape(keys, HD)
        scores = jnp.dot(k4, qt[:, cols], preferred_element_type=F32)
        high = None
        for slot in range(4):
            mask = bias[slot]
            part = scores[slot * HD : (slot + 1) * HD] + jnp.concatenate((mask, mask), axis=1)
            pr[quad, slot] = part
            top = fold(part, jnp.max)
            high = top if high is None else jnp.maximum(high, top)
        high = jnp.max(high, axis=0, keepdims=True)
        dpr[quad] = jnp.dot(v4, dot[:, cols], preferred_element_type=F32).reshape(4, HD, 2 * HD)
        low = None
        for slot in range(4):
            part = jnp.exp((pr[quad, slot] - high) * SCALE)
            pr[quad, slot] = part
            add = fold(part, jnp.sum)
            low = add if low is None else low + add
        mr[quad, half] = jnp.broadcast_to(high, (8, 2 * HD))
        lr[quad, half] = jnp.broadcast_to(jnp.sum(low, axis=0, keepdims=True), (8, 2 * HD))

    def prompt_ready(g):
        gc_copy(g).wait_recv()
        all_rows = gat[:, :, g].reshape(4 * nz, 16, HD).astype(F32)
        kp[g] = all_rows[:, 0:8].reshape(npr, HD).astype(BF)
        vp[g] = all_rows[:, 8:16].reshape(npr, HD).astype(BF)
        for slot in range(4):
            kt[g, :, slot * HD : (slot + 1) * HD] = win[g, slot, 0:HD, :].T
        for lower in range(0, npr, HD):
            kt[g, :, keys + lower : keys + lower + HD] = kp[g, lower : lower + HD, :].T

    chunks = npr // HD

    def full_half(quad, half, pr, dpr, sp, dpp):
        g = lax.div(quad, 2)
        cols = half_cols(quad, half)
        own = slice(half * 2 * HD, (half + 1) * 2 * HD)
        scores = jnp.dot(kp[g], qt[:, cols], preferred_element_type=F32)
        sp[...] = scores
        high = jnp.maximum(mr[quad, half], fold(scores, jnp.max))
        dpp[...] = jnp.dot(vp[g], dot[:, cols], preferred_element_type=F32)
        old = mr[quad, half][0:1]
        high = jnp.max(high, axis=0, keepdims=True)
        low = None
        for c in range(chunks):
            rows = slice(c * HD, (c + 1) * HD)
            part = jnp.exp((sp[rows, :] - high) * SCALE)
            sp[rows, :] = part
            add = fold(part, jnp.sum)
            low = add if low is None else low + add
        shrink = jnp.exp((old - high) * SCALE)
        sums = jnp.sum(low, axis=0, keepdims=True) + lr[quad, half][0:1] * shrink
        f_prompt = 1.0 / sums
        f_resp = shrink * f_prompt
        delta = None
        for slot in range(4):
            rounded = (pr[quad, slot] * f_resp).astype(BF)
            pt[slot * HD : (slot + 1) * HD, own] = rounded
            add = fold(rounded.astype(F32) * dpr[quad, slot], jnp.sum)
            delta = add if delta is None else delta + add
        for c in range(chunks):
            rows = slice(c * HD, (c + 1) * HD)
            rounded = (sp[rows, :] * f_prompt).astype(BF)
            pt[keys + c * HD : keys + (c + 1) * HD, own] = rounded
            delta = delta + fold(rounded.astype(F32) * dpp[rows, :], jnp.sum)
        delta = jnp.sum(delta, axis=0, keepdims=True)
        for slot in range(4):
            dst[quad, slot * HD : (slot + 1) * HD, own] = (
                (pr[quad, slot] * f_resp) * (dpr[quad, slot] - delta)
            ).astype(BF)
        for c in range(chunks):
            rows = slice(c * HD, (c + 1) * HD)
            dst[quad, keys + c * HD : keys + (c + 1) * HD, own] = (
                (sp[rows, :] * f_prompt) * (dpp[rows, :] - delta)
            ).astype(BF)

    def full_quad(quad):
        full_half(quad, 0, pr_a, dpr_a, sp_a, dpp_a)
        full_half(quad, 1, pr_b, dpr_b, sp_b, dpp_b)

    def rows_of(ref, quad):
        part = ref[:, quad_cols(quad)]
        return jnp.concatenate([part[:, i * HD : (i + 1) * HD] for i in range(4)], axis=0)

    def add_keys(quad, lower, upper):
        second = lax.rem(quad, 2) == 1
        rows = slice(lower, upper)
        for acc, left, right in ((dv_acc, pt, do_ref), (dk_acc, dst.at[quad], q_ref)):
            part = jnp.dot(left[rows, :], rows_of(right, quad), preferred_element_type=F32)
            acc[rows, :] = jnp.where(second, acc[rows, :], 0.0) + part

    def query_part(quad):
        g = lax.div(quad, 2)
        part = jnp.dot(kt[g], dst[quad], preferred_element_type=F32)
        dq_ref[:, quad_cols(quad)] = jnp.concatenate(
            [(part[:, i * HD : (i + 1) * HD].T * SCALE).astype(BF) for i in range(4)], axis=1
        )

    def query_out(quad):
        cols = quad_cols(quad)
        return pltpu.make_async_copy(dq_ref.at[:, cols], dq_hbm.at[:, cols], s_out.at[quad])

    def emit_prompt(g):
        dk = dk_acc[keys:total, :] * SCALE
        dv = dv_acc[keys:total, :]
        both = jnp.concatenate(
            (dk.reshape(4 * nz, 8, HD), dv.reshape(4 * nz, 8, HD)), axis=1
        )
        pf[g] = both
        ps[g] = both.astype(BF)
        pc_copy(g).start()

    def emit_resp(g):
        for slot in range(4):
            rows = slice(slot * HD, (slot + 1) * HD)
            dk = dk_acc[rows, :] * SCALE
            dv = dv_acc[rows, :]
            if slot in (0, 2):
                tf[g, slot // 2, 0:HD, :] = dk
                tf[g, slot // 2, HD : 2 * HD, :] = dv
            else:
                tb[g, slot // 2, 0:HD, :] = dk.astype(BF)
                tb[g, slot // 2, HD : 2 * HD, :] = dv.astype(BF)
        tp_copy(g).start()
        tb_copy(g).start()

    half_blocks = 2 * nz

    def pc_copy(g):
        return copy(
            ps.at[g, pl.ds((1 - core) * half_blocks, half_blocks)], rc.at[g], PC, g, peer
        )

    def px_copy(g):
        return copy(xs.at[g], rx.at[g], PX, g, xpeer)

    def px_send(g):
        pc_copy(g).wait_recv()
        away = 1 - x
        xs[g] = (
            pf[g, pl.ds(core * half_blocks + away * nz, nz)]
            + rc[g, pl.ds(away * nz, nz)].astype(F32)
        ).astype(BF)
        xf[g] = (
            pf[g, pl.ds(core * half_blocks + x * nz, nz)] + rc[g, pl.ds(x * nz, nz)].astype(F32)
        )
        px_copy(g).start()

    def near(g, d, slot):
        return copy(zs.at[g, lax.rem(z + d, nz)], rz.at[g, slot], PZ, g, zpeer(d))

    def far(g, d, by, slot):
        return copy(zs.at[g, lax.rem(z + d, nz)], ry.at[g, slot], PY, g, zpeer(by))

    def relay(g, d, slot):
        return copy(ys.at[g, slot], rz.at[g, 6 + slot], PW, g, zpeer(d))

    def pz_send(g):
        px_copy(g).wait_recv()
        sums = xf[g] + rx[g].astype(F32)
        zf[g] = sums
        zs[g] = sums.astype(BF)
        for k in range(1, 5):
            far(g, nz - 4 - k, nz - k, k - 1).start()
        for k in range(1, 4):
            far(g, 4 + k, k, 3 + k).start()
        for k in range(1, 4):
            near(g, k, k - 1).start()
            near(g, nz - k, 2 + k).start()

    def far_all(g):
        return copy(zs.at[g, pl.ds(0, 7)], ry.at[g], PY, g, peer)

    def near_all(g):
        return copy(zs.at[g, pl.ds(0, 6)], rz.at[g, pl.ds(0, 6)], PZ, g, peer)

    def relay_all(g):
        return copy(ys.at[g], rz.at[g, pl.ds(6, 2)], PW, g, peer)

    def pw_send(g):
        far_all(g).wait_recv()
        below = zf[g, lax.rem(z + nz - 4, nz)] + jnp.sum(ry[g, 0:4].astype(F32), axis=0)
        above = zf[g, lax.rem(z + 4, nz)] + jnp.sum(ry[g, 4:7].astype(F32), axis=0)
        ys[g, 0] = below.astype(BF)
        ys[g, 1] = above.astype(BF)
        relay(g, nz - 4, 0).start()
        relay(g, 4, 1).start()

    def prompt_out(g):
        near_all(g).wait_recv()
        relay_all(g).wait_recv()
        sums = zf[g, z] + jnp.sum(rz[g].astype(F32), axis=0)
        cols = slice(g * HD, (g + 1) * HD)
        dpk_ref[:, cols] = sums[0:8]
        dpv_ref[:, cols] = sums[8:16]

    def tp_copy(g):
        return copy(tb.at[g, core], rp.at[g], TP, g, peer)

    def tb_copy(g):
        return copy(tb.at[g, 1 - core], rb.at[g], TB, g, lax.rem(me + n - 3 + 2 * core, n))

    def ta_copy(g):
        return copy(ts.at[g], ra.at[g], TA, g, lax.rem(me + n - 2, n))

    def ts_send(g):
        tp_copy(g).wait_recv()
        ts[g] = (tf[g, 1] + rp[g].astype(F32)).astype(BF)
        ta_copy(g).start()

    def resp_out(g):
        ta_copy(g).wait_recv()
        tb_copy(g).wait_recv()
        sums = tf[g, 0] + ra[g].astype(F32) + rb[g].astype(F32)
        cols = slice(g * HD, (g + 1) * HD)
        drk_ref[:, cols] = sums[0:HD]
        drv_ref[:, cols] = sums[HD : 2 * HD]

    def when(flag, *calls):
        @pl.when(flag)
        def _():
            for call, g in calls:
                call(g)

    def resp_quad(quad):
        resp_half(quad, 0, pr_a, dpr_a)
        resp_half(quad, 1, pr_b, dpr_b)

    kv_ready(0)
    make_bias()

    def resp_step(quad, carry):
        when(quad == 2, (kv_ready, 1))
        resp_quad(quad)
        when(quad == 0, (ring_step, 4), (kv_forward, 1), (kv_send, 3))

        @pl.when(quad == 1)
        def _():
            ring_end()
            for g in range(HK):
                gather_x(g)

        when(quad == 2, (kv_forward, 2))
        when(quad == 3, (gather_c, 0))
        return carry

    lax.fori_loop(0, 4, resp_step, 0)
    kv_ready(2)
    prompt_ready(0)
    resp_quad(4)
    full_quad(0)
    gather_c(1)

    def both_step(quad, carry):
        when(quad == 6, (kv_ready, 3), (prompt_ready, 1))
        add_keys(quad - 5, 0, total)
        resp_quad(quad)
        full_quad(quad - 4)
        when(quad == 5, (kv_forward, 3))
        when(quad == 6, (emit_prompt, 0), (emit_resp, 0), (gather_c, 2))
        when(quad == 7, (gather_c, 3), (px_send, 0), (ts_send, 0))
        return carry

    lax.fori_loop(5, quads, both_step, 0)

    def full_step(quad, carry):
        g = lax.div(quad, 2)
        first = lax.rem(quad, 2) == 0
        when(first, (prompt_ready, g))
        add_keys(quad - 1, 0, total)
        full_quad(quad)
        when(first, (emit_prompt, g - 1), (emit_resp, g - 1), (pz_send, g - 2))
        when(~first, (px_send, g - 1), (ts_send, g - 1), (pw_send, g - 2))
        return carry

    lax.fori_loop(4, quads, full_step, 0)

    def query(*which):
        for quad in which:
            query_part(quad)
            query_out(quad).start()

    last = HK - 1
    add_keys(quads - 1, keys, total)
    emit_prompt(last)
    add_keys(quads - 1, 0, keys)
    emit_resp(last)
    pz_send(last - 1)
    query(0, 1, 2)
    px_send(last)
    ts_send(last)
    query(3, 4)
    pw_send(last - 1)
    query(5)
    pz_send(last)
    query(6, 7)
    for g in range(last):
        prompt_out(g)
        resp_out(g)
    pw_send(last)
    resp_out(last)
    prompt_out(last)

    sent = gat.at[0, 0, pl.ds(0, HK), pl.ds(0, nz - 1)]
    pltpu.make_async_remote_copy(
        src_ref=sent,
        dst_ref=sent,
        send_sem=s_ring.at[0],
        recv_sem=r_ring.at[0],
        device_id=device(peer),
        device_id_type=MESH,
    ).wait_send()
    for g in range(HK):
        kv_far(g).wait_send()
        kv_side(g).wait_send()
        kv_pass(g).wait_send()
        gx_copy(g).wait_send()
        gc_copy(g).wait_send()
        pc_copy(g).wait_send()
        px_copy(g).wait_send()
        near_all(g).wait_send()
        far_all(g).wait_send()
        relay_all(g).wait_send()
        tp_copy(g).wait_send()
        tb_copy(g).wait_send()
        ta_copy(g).wait_send()
    for quad in range(quads):
        query_out(quad).wait()


PIECES = ((0, 4), (1, 1), (2, 1), (3, 1), (4, 1))


def hand_over(*refs):
    sources, targets, held, sems = refs[:5], refs[5:10], refs[10:15], refs[15]
    loads, stores = [], []
    for index, count in PIECES:
        rows = sources[index].shape[0] // count
        for i in range(count):
            part = pl.ds(i * rows, rows)
            here = held[index].at[part]
            slot = len(loads)
            loads.append(
                pltpu.make_async_copy(sources[index].at[part], here, sems.at[0, slot])
            )
            stores.append(
                pltpu.make_async_copy(here, targets[index].at[part], sems.at[1, slot])
            )
    for load in loads:
        load.start()
    for load, store in zip(loads, stores):
        load.wait()
        store.start()
    for store in stores:
        store.wait()


def on_device(queries, resp_key, resp_value, prompt_key, prompt_value, out_grad, segment):
    n = lax.axis_size("seq")
    nz = n // 4
    rows = queries.shape[0]
    npr = 32 * nz
    total = 4 * HD + npr
    quads = 2 * HK
    vmem = pl.BlockSpec(memory_space=pltpu.VMEM)
    whole = pl.BlockSpec(memory_space=pl.ANY)
    flat = HK * GROUP * HD
    scratch = [
        ((rows, HK * HD), BF),
        ((rows, HK * HD), BF),
        ((8, HK * HD), BF),
        ((8, HK * HD), BF),
        ((1, rows), jnp.int32),
        ((rows, flat), BF),
        ((rows, flat), BF),
        ((rows, flat), BF),
        ((HD, flat), BF),
        ((HD, flat), BF),
        ((HK, 4, 2 * HD + 16, HD), BF),
        ((2, 2, HK, nz, 16, HD), BF),
        ((4, HD, HD), F32),
        ((quads, 4, HD, 2 * HD), F32),
        ((quads, 4, HD, 2 * HD), F32),
        ((quads, 4, HD, 2 * HD), F32),
        ((quads, 4, HD, 2 * HD), F32),
        ((quads, 2, 8, 2 * HD), F32),
        ((quads, 2, 8, 2 * HD), F32),
        ((npr, 2 * HD), F32),
        ((npr, 2 * HD), F32),
        ((npr, 2 * HD), F32),
        ((npr, 2 * HD), F32),
        ((HK, npr, HD), BF),
        ((HK, npr, HD), BF),
        ((HK, HD, total), BF),
        ((total, 4 * HD), BF),
        ((quads, total, 4 * HD), BF),
        ((total, HD), F32),
        ((total, HD), F32),
        ((HK, 4 * nz, 16, HD), BF),
        ((HK, 4 * nz, 16, HD), F32),
        ((HK, 2 * nz, 16, HD), BF),
        ((HK, nz, 16, HD), BF),
        ((HK, nz, 16, HD), F32),
        ((HK, nz, 16, HD), BF),
        ((HK, nz, 16, HD), BF),
        ((HK, nz, 16, HD), F32),
        ((HK, 8, 16, HD), BF),
        ((HK, 7, 16, HD), BF),
        ((HK, 2, 16, HD), BF),
        ((HK, 2, 2 * HD, HD), BF),
        ((HK, 2, 2 * HD, HD), F32),
        ((HK, 2 * HD, HD), BF),
        ((HK, 2 * HD, HD), BF),
        ((HK, 2 * HD, HD), BF),
        ((HK, 2 * HD, HD), BF),
    ]
    shapes = [
        jax.ShapeDtypeStruct((rows, flat), BF),
        jax.ShapeDtypeStruct((rows, HK * HD), F32),
        jax.ShapeDtypeStruct((rows, HK * HD), F32),
        jax.ShapeDtypeStruct((8, HK * HD), F32),
        jax.ShapeDtypeStruct((8, HK * HD), F32),
    ]
    results = pl.pallas_call(
        lambda *refs: body(nz, *refs),
        out_shape=shapes,
        in_specs=[whole] * 7,
        out_specs=[whole] + [vmem] * 4,
        scratch_shapes=[pltpu.VMEM(shape, kind) for shape, kind in scratch]
        + [
            pltpu.SemaphoreType.DMA((HK, 3)),
            pltpu.SemaphoreType.DMA((HK, 4)),
            pltpu.SemaphoreType.DMA((1,)),
            pltpu.SemaphoreType.DMA((nz,)),
            pltpu.SemaphoreType.DMA((10, HK)),
            pltpu.SemaphoreType.DMA((10, HK)),
            pltpu.SemaphoreType.DMA((7,)),
            pltpu.SemaphoreType.DMA((quads,)),
        ],
        compiler_params=pltpu.CompilerParams(
            collective_id=0, has_side_effects=True, vmem_limit_bytes=60 * 1024 * 1024
        ),
        cost_estimate=pl.CostEstimate(
            flops=6 * 10**9, bytes_accessed=6 * 10**6, transcendentals=4 * 10**6
        ),
        name="attention_backward",
    )(
        queries,
        resp_key,
        resp_value,
        prompt_key,
        prompt_value,
        out_grad,
        segment.reshape(1, rows),
    )
    return tuple(
        pl.pallas_call(
            hand_over,
            out_shape=shapes,
            in_specs=[whole] * 5,
            out_specs=[whole] * 5,
            scratch_shapes=[pltpu.VMEM(one.shape, one.dtype) for one in shapes]
            + [pltpu.SemaphoreType.DMA((2, sum(count for _, count in PIECES)))],
            compiler_params=pltpu.CompilerParams(vmem_limit_bytes=60 * 1024 * 1024),
            cost_estimate=pl.CostEstimate(
                flops=0, bytes_accessed=3 * 10**6, transcendentals=0
            ),
            name="hand_over",
        )(*results)
    )


def solution(mesh):
    spec = P(("grp", "seq"), None)
    return jax.shard_map(
        on_device,
        mesh=mesh,
        in_specs=(spec,) * 6 + (P(("grp", "seq")),),
        out_specs=(spec,) * 5,
        check_vma=False,
    )
```
